128 devices in a mesh: fsdp: 64 (over z, x, y), layer: 2 (over core).
Axes of the slice: x: 4, y: 4, z: 4, core: 2. Of those that a mesh axis runs over, the one named last changes fastest.
Arguments:
- gradients: bfloat16 [4, 5120, 25600], P('layer', 'fsdp')
- sketch: bfloat16 [5120, 512], P('fsdp'), may hold values from -0.078125 to 0.078125
- rank_lists: int32 [4, 256], P('layer'), may hold values from 0 to 511, as said below
- old_basis: bfloat16 [4, 25600, 256], P('layer', 'fsdp'), may hold values from -6 to 6
- first_moment: float32 [4, 5120, 256], P('layer', 'fsdp'), may hold values from -6 to 6
- second_moment: float32 [4, 5120, 256], P('layer', 'fsdp'), may hold values from 0.1 to 4
Outputs:
- new_basis: bfloat16 [4, 25600, 256], P('layer', 'fsdp')
- projected: bfloat16 [4, 5120, 256], P('layer', 'fsdp')
- moment_one: float32 [4, 5120, 256], P('layer', 'fsdp')
- moment_two: float32 [4, 5120, 256], P('layer', 'fsdp')
- scores: float32 [512], replicated
The draws below stay inside these ranges and needn't reach their ends.
Inputs may be any that keep to these rules, and one draw needn't show every extreme that they name: `rank_lists`: each row holds 256 different column numbers, among them 0 and 511.
All inputs are finite; a program needn't handle non-finite values.
Results may differ from the reference program's by a relative error of at most 0.0065.
Values may be sent and summed in bfloat16 or wider, within the bound.
No kernel may reach another device: no remote copies, remote signals or barrier semaphores. Data moves between devices by JAX's collectives and lax.ppermute only.
A program may use at most 128 MiB of HBM per device.

```python
import math
import jax
import jax.numpy as jnp
from jax import lax

D = 5120
FF = 25600
KS = 512
RANK = 256
LAYERS = 4
N_FSDP = 64


def draw_rank_lists(key, part):
    key = jax.random.fold_in(key, 7)
    layer_keys = jax.random.split(key, LAYERS)

    def choose_one(one_key):
        left_key, right_key = jax.random.split(one_key)
        middle = (jax.random.permutation(left_key, KS - 2) + 1).astype(jnp.int32)
        chosen = jnp.concatenate([jnp.array([0, KS - 1], dtype=jnp.int32), middle[:RANK - 2]])
        return jax.random.permutation(right_key, chosen).astype(jnp.int32)
    return jax.vmap(choose_one)(layer_keys)


def draw_gradients(key, part):
    key = jax.random.fold_in(key, 11)
    base_key, pair_key = jax.random.split(key)
    base = jnp.clip(jax.random.normal(base_key, (LAYERS, D, FF), jnp.float32), -6.0, 6.0)
    rise = 2.0
    pairing = jax.random.permutation(pair_key, N_FSDP).astype(jnp.int32)
    row_block = (jnp.arange(D, dtype=jnp.int32) // (D // N_FSDP)).astype(jnp.int32)
    col_block = (jnp.arange(FF, dtype=jnp.int32) // (FF // N_FSDP)).astype(jnp.int32)
    paired = pairing[col_block]
    spike = jnp.where(paired[None, :] == row_block[:, None], 3.0, 1.0).astype(jnp.float32)
    layer_pos = jnp.arange(LAYERS, dtype=jnp.float32) / max(LAYERS - 1, 1)
    layer_scale = jnp.sqrt(1.0 + rise * layer_pos)
    return (base * spike[None, :, :] * layer_scale[:, None, None]).astype(jnp.bfloat16)


def level_of(key, dims, pieces, least, high):
    factor_of, own = 1.0, jax.random.fold_in(key, 6)
    for axis_at, parts in pieces:
        steps = jnp.exp(jax.random.uniform(jax.random.fold_in(own, axis_at), (parts,), jnp.float32, least / len(pieces), high / len(pieces)))
        factor_of = factor_of * jnp.repeat(steps, dims[axis_at] // parts).reshape([-1 if axis == axis_at else 1 for axis in range(len(dims))])
    return factor_of


def noise(key, dims, width, bound, cuts=(), kind=jnp.bfloat16):
    gain = level_of(key, dims, cuts, -0.22, 0.18) if cuts else 1.0
    entries = jax.random.normal(key, dims, jnp.float32) * width * gain
    return jnp.minimum(jnp.maximum(entries, -bound), bound).astype(kind)


def setup_inputs(seed: int = 0) -> dict:
    key_list = jax.random.split(jax.random.key(seed), 7)
    gradients = draw_gradients(jax.random.fold_in(key_list[6], 71), 0)
    sketch = noise(key_list[1], (D, KS), D ** -0.5, 0.078125, ((0, 64),))
    rank_lists = draw_rank_lists(jax.random.fold_in(key_list[6], 71), 0)
    old_basis = noise(key_list[3], (LAYERS, FF, RANK), 1.0, 6.0, ((0, 2), (1, 64)))
    first_moment = noise(key_list[4], (LAYERS, D, RANK), 1.0, 6.0, ((0, 2), (1, 64)), jnp.float32)
    second_moment = jnp.clip(jnp.exp(math.log(4.0) - 3.6888794 * jax.random.uniform(key_list[5], (LAYERS, D, RANK), jnp.float32) ** level_of(key_list[5], (LAYERS, D, RANK), ((0, 2), (1, 64)), -0.2, 0.2)), 0.1, 4.0)
    return {"gradients": gradients, "sketch": sketch, "rank_lists": rank_lists, "old_basis": old_basis, "first_moment": first_moment, "second_moment": second_moment}


highest = lax.Precision.HIGHEST

def refresh_layer(gradient, sketch, chosen, previous, moment_first, moment_second):
    sketched = jnp.dot(gradient.T, sketch, preferred_element_type=jnp.float32).astype(jnp.bfloat16)
    gram = jnp.dot(sketched.T, sketched, preferred_element_type=jnp.float32)
    trace_sum = jnp.sum(jnp.diagonal(gram))
    unit_matrix = jnp.eye(KS, dtype=jnp.float32)
    corrected = 1.5 * unit_matrix - 0.5 * KS / trace_sum * gram
    scale_rms = jnp.sqrt(trace_sum / (FF * KS))
    factor = (jnp.take(corrected, chosen, axis=1) / scale_rms).astype(jnp.bfloat16)
    basis_full = jnp.dot(sketched, factor, preferred_element_type=jnp.float32)
    basis_new = basis_full.astype(jnp.bfloat16)
    correlation = jnp.dot(previous.astype(jnp.float32).T, basis_full, precision=highest) / math.sqrt(FF * RANK)
    projected = (jnp.dot(gradient, basis_new, preferred_element_type=jnp.float32) / math.sqrt(FF)).astype(jnp.bfloat16)
    moment_new = jnp.dot(moment_first, correlation, precision=highest)
    moment_sq = jnp.dot(moment_second, correlation * correlation, precision=highest)
    layer_scores = jnp.diagonal(gram) / FF
    return (basis_new, projected, moment_new, moment_sq, layer_scores)

def reference(gradients, sketch, rank_lists, old_basis, first_moment, second_moment):

    def single(inputs):
        return refresh_layer(inputs[0], sketch, inputs[1], inputs[2], inputs[3], inputs[4])
    basis_new, projected, moment_new, moment_sq, layer_scores = lax.map(single, (gradients, rank_lists, old_basis, first_moment, second_moment))
    return (basis_new, projected, moment_new, moment_sq, lax.optimization_barrier(jnp.sum(layer_scores, axis=0)))
```

```python
import math

import jax
import jax.numpy as jnp
from jax import lax
from jax.experimental import pallas as pl
from jax.experimental.pallas import tpu as pltpu
from jax.sharding import Mesh, PartitionSpec as P

FF = 25600
KS = 512
RANK = 256
ROWS = 80
COLS = 400
NL = 2
N = 64

bf16 = jnp.bfloat16
f32 = jnp.float32
highest = lax.Precision.HIGHEST
AX = ("z", "x", "y")
VMEM = 48 * 1024 * 1024


def pack_kernel(g_ref, a_ref, b_ref, c_ref):
    for j in range(8):
        for l in range(NL):
            v = g_ref[l, :, COLS * j : COLS * (j + 1)]
            rows = pl.ds(ROWS * l, ROWS)
            a_ref[j, rows, :] = v[:, 0:128]
            b_ref[j, rows, :] = v[:, 128:256]
            c_ref[j, rows, :] = v[:, 256:384]
            rest = v[:, 384:400]
            tail = jnp.concatenate(
                [rest[16 * g : 16 * g + 16] for g in range(5)] + [jnp.zeros((16, 48), bf16)], axis=1
            )
            dst = a_ref if l == 0 else b_ref
            dst[j, 160:176, :] = tail


def pack(g):
    def out(n):
        return jax.ShapeDtypeStruct((N, n, 128), bf16)

    def spec(n):
        return pl.BlockSpec((8, n, 128), lambda i: (i, 0, 0))

    return pl.pallas_call(
        pack_kernel,
        grid=(8,),
        in_specs=[pl.BlockSpec((NL, ROWS, 8 * COLS), lambda i: (0, 0, i))],
        out_specs=[spec(176), spec(176), spec(160)],
        out_shape=[out(176), out(176), out(160)],
        compiler_params=pltpu.CompilerParams(vmem_limit_bytes=VMEM),
        cost_estimate=pl.CostEstimate(flops=0, bytes_accessed=17_000_000, transcendentals=0),
    )(g)


def assemble_kernel(a_ref, b_ref, c_ref, x_ref):
    for i in range(4):
        for l in range(NL):
            src = pl.ds(ROWS * l, ROWS)
            dst = pl.ds(ROWS * i, ROWS)
            x_ref[l, dst, 0:128] = a_ref[i, src, :]
            x_ref[l, dst, 128:256] = b_ref[i, src, :]
            x_ref[l, dst, 256:384] = c_ref[i, src, :]
            tail = (a_ref if l == 0 else b_ref)[i, 160:176, :]
            for g in range(5):
                piece = tail[:, 16 * g : 16 * g + 16]
                x_ref[l, pl.ds(ROWS * i + 16 * g, 16), 384:512] = jnp.concatenate(
                    [piece, jnp.zeros((16, 112), bf16)], axis=1
                )


def assemble(a, b, c):
    def spec(n):
        return pl.BlockSpec((4, n, 128), lambda i: (i, 0, 0))

    return pl.pallas_call(
        assemble_kernel,
        grid=(N // 4,),
        in_specs=[spec(176), spec(176), spec(160)],
        out_specs=pl.BlockSpec((NL, 4 * ROWS, 512), lambda i: (0, i, 0)),
        out_shape=jax.ShapeDtypeStruct((NL, N * ROWS, 512), bf16),
        compiler_params=pltpu.CompilerParams(vmem_limit_bytes=VMEM),
        cost_estimate=pl.CostEstimate(flops=0, bytes_accessed=19_000_000, transcendentals=0),
    )(a, b, c)


def shifted(x, axis, k):
    return lax.ppermute(x, axis, [(s, (s - k) % 4) for s in range(4)])


def pick(buf, index, dim):
    return lax.dynamic_index_in_dim(buf, index, dim, keepdims=False)


def dest(axis, k):
    return lax.rem(lax.axis_index(axis) + (4 - k), 4)


ORDERS = (("z", "x", "y"), ("x", "y", "z"), ("y", "z", "x"))
ISSUE = ((0, 2), (1, 2), (2, 1), (2, 3), (0, 1), (1, 1), (1, 3), (0, 3), (2, 2))


def exchange(bufs):
    state = []
    for t, buf in enumerate(bufs):
        cube = buf.reshape((4, 4, 4) + buf.shape[1:])
        state.append([cube])
    for stage in range(3):
        got = [[None] * 4 for _ in range(3)]

        def piece(t, k):
            axis = ORDERS[t][stage]
            if stage == 0:
                return pick(state[t][0], dest(axis, k), AX.index(axis))
            left = [a for a in AX if a in ORDERS[t][stage:]]
            dim = (stage - 1) + left.index(axis)
            return jnp.stack([pick(p, dest(axis, k), dim) for p in state[t]], 0)

        for t in range(3):
            got[t][0] = piece(t, 0)
        for t, k in ISSUE:
            got[t][k] = shifted(piece(t, k), ORDERS[t][stage], k)
        state = got
    outs = []
    for t in range(3):
        full = jnp.stack(state[t], 0)
        names = ORDERS[t][::-1]
        full = full.transpose([names.index(a) for a in AX] + [3, 4])
        outs.append(full.reshape((N,) + full.shape[3:]))
    return outs


def reduce_scatter(parts):
    state = list(parts)
    for stage in range(3):
        got = [[None] * 4 for _ in range(3)]

        def piece(t, k):
            left = [a for a in AX if a in ORDERS[t][stage:]]
            return lax.index_in_dim(state[t], k, left.index(ORDERS[t][stage]), keepdims=False)

        for t in range(3):
            got[t][0] = piece(t, 0)
        for t, k in ISSUE:
            got[t][k] = shifted(piece(t, (4 - k) % 4), ORDERS[t][stage], k)
        state = []
        for t in range(3):
            total = sum(p.astype(f32) for p in got[t])
            state.append(total if stage == 2 else total.astype(bf16))
    return state


def gather_rows(x):
    for axis in ("y", "x", "z"):
        pieces = [x] + [shifted(x, axis, k) for k in (1, 2, 3)]
        twice = jnp.stack(pieces + pieces[:3], 0)
        x = lax.dynamic_slice_in_dim(twice, lax.rem(4 - lax.axis_index(axis), 4), 4, 0)
    return x.reshape((N,) + x.shape[3:])


def relative(s):
    cube = s.reshape((4, 4, 4) + s.shape[1:])
    for dim, axis in enumerate(AX):
        twice = jnp.concatenate([cube, lax.slice_in_dim(cube, 0, 3, axis=dim)], dim)
        cube = lax.dynamic_slice_in_dim(twice, lax.axis_index(axis), 4, dim)
    return cube


def shards(gradients, sketch, rank_lists, old_basis, first_moment, second_moment):
    full_sketch = lax.all_gather(sketch, AX, axis=0, tiled=True)
    panels = assemble(*exchange(pack(gradients)))
    s_rel = relative(full_sketch.reshape(N, ROWS, KS)).reshape(N * ROWS, KS)

    sketched = []
    sums = []
    diags = []
    projections = []
    for l in range(NL):
        sk = lax.dot_general(
            panels[l], s_rel, (((0,), (0,)), ((), ())), preferred_element_type=f32
        ).astype(bf16)
        picker = (lax.broadcasted_iota(jnp.int32, (KS, RANK), 0) == rank_lists[l][None, :]).astype(bf16)
        chosen_cols = jnp.dot(sk, picker, preferred_element_type=f32).astype(bf16)
        old = jnp.pad(old_basis[l], ((0, KS - COLS), (0, 0)))
        right = jnp.concatenate([chosen_cols, old], 1)
        sums.append(
            lax.dot_general(sk, right, (((0,), (0,)), ((), ())), preferred_element_type=f32).astype(bf16)
        )
        wide = sk.astype(f32)
        diags.append(jnp.sum(wide * wide, axis=0))
        projections.append(jnp.dot(panels[l], sk, preferred_element_type=f32).astype(bf16))
        sketched.append(sk)

    diag = jnp.stack(diags, 0)
    high = diag.astype(bf16)
    rest = diag - high.astype(f32)
    mid = rest.astype(bf16)
    low = (rest - mid.astype(f32)).astype(bf16)
    pieces = jnp.concatenate([high, mid, low, jnp.zeros((2, KS), bf16)], 0)
    blocks = jnp.stack(sums, 0).reshape(NL, N, 8, KS).transpose(1, 0, 2, 3).reshape(N, NL * 8, KS)
    send = jnp.concatenate([blocks, jnp.broadcast_to(pieces[None], (N, 8, KS))], 1)
    got = lax.all_to_all(send, AX, 0, 0, tiled=True)
    total = jnp.sum(got.astype(f32), axis=0)
    row_sums = total[: NL * 8].reshape(NL, 8, KS)
    diag = total[16:18] + total[18:20] + total[20:22]
    trace = jnp.sum(diag, axis=1)

    me = (lax.axis_index("z") * 4 + lax.axis_index("x")) * 4 + lax.axis_index("y")
    my_rows = me * 8 + lax.broadcasted_iota(jnp.int32, (8, RANK), 0)
    owned = []
    for l in range(NL):
        scale = 0.5 * KS / trace[l]
        rms = jnp.sqrt(trace[l] / (FF * KS))
        my_diag = lax.dynamic_slice_in_dim(diag[l], me * 8, 8, 0)[:, None]
        corrected = jnp.where(
            my_rows == rank_lists[l][None, :], 1.5 - scale * my_diag, -scale * row_sums[l][:, :RANK]
        )
        owned.append(
            jnp.concatenate([(corrected / rms).astype(bf16), row_sums[l][:, RANK:].astype(bf16)], 1)
        )
    everyone = gather_rows(jnp.stack(owned, 0))

    t_all = jnp.stack(projections, 0).reshape(NL, 4, 4, 4, ROWS, KS)
    t_all = t_all.transpose(1, 2, 3, 0, 4, 5).reshape(4, 4, 4, NL * ROWS, KS)
    t_parts = reduce_scatter([t_all[..., 0:56, :], t_all[..., 56:112, :], t_all[..., 112:160, :]])
    t_rows = jnp.concatenate(t_parts, 0).reshape(NL, ROWS, KS)

    basis_list, projected_list, first_list, second_list = [], [], [], []
    for l in range(NL):
        both = everyone[:, l].reshape(KS, KS)
        factor, inner = both[:, :RANK], both[:, RANK:]
        basis_list.append(
            jnp.dot(sketched[l][:COLS], factor, preferred_element_type=f32).astype(bf16)
        )
        correlation = lax.dot_general(
            inner, factor, (((0,), (0,)), ((), ())), preferred_element_type=f32
        ) / math.sqrt(FF * RANK)
        projected_list.append(
            (jnp.dot(t_rows[l], factor.astype(f32), precision=highest) / math.sqrt(FF)).astype(bf16)
        )
        first_list.append(jnp.dot(first_moment[l], correlation, precision=highest))
        second_list.append(jnp.dot(second_moment[l], correlation * correlation, precision=highest))
    scores = lax.psum((diag[0] + diag[1]) / FF, "layer")
    return (
        jnp.stack(basis_list, 0),
        jnp.stack(projected_list, 0),
        jnp.stack(first_list, 0),
        jnp.stack(second_list, 0),
        scores,
    )


def solution(mesh):
    cube = Mesh(mesh.devices.reshape(4, 4, 4, 2), AX + ("layer",))
    rows = P("layer", AX, None)
    return jax.shard_map(
        shards,
        mesh=cube,
        in_specs=(rows, P(AX, None), P("layer", None), rows, rows, rows),
        out_specs=(rows, rows, rows, rows, P()),
        check_vma=False,
    )
```

```python
import math

import jax
import jax.numpy as jnp
from jax import lax
from jax.experimental import pallas as pl
from jax.experimental.pallas import tpu as pltpu
from jax.sharding import Mesh, PartitionSpec as P

FF = 25600
KS = 512
RANK = 256
ROWS = 80
COLS = 400
NL = 2
N = 64

bf16 = jnp.bfloat16
f32 = jnp.float32
highest = lax.Precision.HIGHEST
AX = ("z", "x", "y")
VMEM = 56 * 1024 * 1024

ORDERS = (("z", "x", "y"), ("x", "y", "z"), ("y", "z", "x"))
PANEL = (176, 176, 160)
BACK = (208, 208, 224)
ISSUE = (
    ((0, 2), (1, 2), (2, 1), (2, 3), (2, 2), (0, 1), (0, 3), (1, 1), (1, 3)),
    ((1, 2), (2, 2), (0, 1), (0, 3), (0, 2), (1, 1), (1, 3), (2, 1), (2, 3)),
    ((2, 2), (0, 2), (1, 1), (1, 3), (1, 2), (2, 1), (2, 3), (0, 1), (0, 3)),
)
HBM = pl.BlockSpec(memory_space=pl.ANY)
SMEM = pl.BlockSpec(memory_space=pltpu.SMEM)
INNER = pl.BlockSpec(memory_space=pltpu.VMEM)


def rest_axes(t, stage):
    return [a for a in AX if a in ORDERS[t][stage:]]


def shifted(x, axis, k):
    return lax.ppermute(x, axis, [(s, (s - k) % 4) for s in range(4)])


def params():
    return pltpu.CompilerParams(vmem_limit_bytes=VMEM)


def cost(nbytes, flops=0):
    return pl.CostEstimate(flops=flops, bytes_accessed=nbytes, transcendentals=0)


def run_copies(copies):
    for c in copies:
        c.start()
    for c in copies:
        c.wait()


def pack_kernel(pos_ref, g_ref, *refs):
    outs, scr, sem = refs[:12], refs[12:15], refs[15]
    g = pl.program_id(0)
    here = [pos_ref[i] for i in range(3)]
    for j in range(8):
        there = [g // 2, 2 * lax.rem(g, 2) + j // 4, j % 4]
        tails = []
        for l in range(NL):
            rest = g_ref[l, :, COLS * j + 384 : COLS * (j + 1)]
            tails.append(
                jnp.concatenate(
                    [rest[16 * i : 16 * i + 16] for i in range(5)] + [jnp.zeros((16, 48), bf16)], axis=1
                )
            )
        for t in range(3):
            first = AX.index(ORDERS[t][0])
            other = [i for i in range(3) if i != first]
            k = lax.rem(here[first] - there[first] + 4, 4)
            at = there[other[0]] * 4 + there[other[1]]
            for l in range(NL):
                scr[t][k, at, pl.ds(ROWS * l, ROWS), :] = g_ref[
                    l, :, COLS * j + 128 * t : COLS * j + 128 * (t + 1)
                ]
            if t < 2:
                scr[t][k, at, pl.ds(160, 16), :] = tails[t]

    @pl.when(g == 7)
    def _():
        run_copies(
            [
                pltpu.make_async_copy(scr[t].at[k], outs[4 * t + k], sem.at[4 * t + k])
                for t in range(3)
                for k in range(4)
            ]
        )


def pack(pos, g):
    outs = pl.pallas_call(
        pack_kernel,
        grid=(8,),
        in_specs=[SMEM, pl.BlockSpec((NL, ROWS, 8 * COLS), lambda i: (0, 0, i))],
        out_specs=[HBM] * 12,
        out_shape=[jax.ShapeDtypeStruct((16, n, 128), bf16) for n in PANEL for _ in range(4)],
        scratch_shapes=[pltpu.VMEM((4, 16, n, 128), bf16) for n in PANEL] + [pltpu.SemaphoreType.DMA((12,))],
        compiler_params=params(),
        cost_estimate=cost(17_000_000),
    )(pos, g)
    return [[o.reshape((4, 4) + o.shape[1:]) for o in outs[4 * t : 4 * t + 4]] for t in range(3)]


def permute_stage(bufs, stage, orders=ISSUE):
    got = [[b[0], None, None, None] for b in bufs]
    for t, k in orders[stage]:
        got[t][k] = shifted(bufs[t][k], ORDERS[t][stage], k)
    return got


def flat(got, stage):
    return [got[t][k] for t, k in ISSUE[stage]] + [got[t][0] for t in range(3)]


def unflat(refs, stage):
    got = [[None] * 4 for _ in range(3)]
    for (t, k), r in zip(ISSUE[stage], refs[:9]):
        got[t][k] = r
    for t in range(3):
        got[t][0] = refs[9 + t]
    return got


def second_kernel(pos_ref, *refs):
    first = unflat(refs[:12], 0)
    outs, sem = refs[12:21], refs[21]
    here = [pos_ref[i] for i in range(3)]
    copies = []
    for at, (t, k) in enumerate(ISSUE[1]):
        axis = ORDERS[t][1]
        place = lax.rem(here[AX.index(axis)] + 4 - k, 4)
        for k1 in range(4):
            src = first[t][k1]
            src = src.at[place] if rest_axes(t, 1).index(axis) == 0 else src.at[:, place]
            copies.append(pltpu.make_async_copy(src, outs[at].at[k1], sem.at[4 * at + k1]))
    run_copies(copies)


def second(pos, got):
    outs = pl.pallas_call(
        second_kernel,
        in_specs=[SMEM] + [HBM] * 12,
        out_specs=[HBM] * 9,
        out_shape=[jax.ShapeDtypeStruct((4, 4, PANEL[t], 128), bf16) for t, _ in ISSUE[1]],
        scratch_shapes=[pltpu.SemaphoreType.DMA((36,))],
        compiler_params=params(),
        cost_estimate=cost(13_000_000),
    )(pos, *flat(got, 0))
    bufs = [[None] * 4 for _ in range(3)]
    for (t, k), o in zip(ISSUE[1], outs):
        bufs[t][k] = o
    return bufs


def third_kernel(pos_ref, *refs):
    first = unflat(refs[:12], 0)
    later = [[None] * 4 for _ in range(3)]
    for (t, k), r in zip(ISSUE[1], refs[12:21]):
        later[t][k] = r
    outs, sem = refs[21:33], refs[33]
    here = [pos_ref[i] for i in range(3)]
    copies = []
    for at, (t, k) in enumerate(ISSUE[2] + ((0, 0), (1, 0), (2, 0))):
        axis2, axis3 = ORDERS[t][1], ORDERS[t][2]
        own = here[AX.index(axis2)]
        place = lax.rem(here[AX.index(axis3)] + 4 - k, 4)
        for k1 in range(4):
            src = first[t][k1]
            src = src.at[own, place] if rest_axes(t, 1).index(axis2) == 0 else src.at[place, own]
            copies.append(pltpu.make_async_copy(src, outs[at].at[0, k1], sem.at[len(copies)]))
        for k2 in range(1, 4):
            copies.append(
                pltpu.make_async_copy(later[t][k2].at[:, place], outs[at].at[k2], sem.at[len(copies)])
            )
    run_copies(copies)


def third(pos, got1, got2):
    order = ISSUE[2] + ((0, 0), (1, 0), (2, 0))
    outs = pl.pallas_call(
        third_kernel,
        in_specs=[SMEM] + [HBM] * 21,
        out_specs=[HBM] * 12,
        out_shape=[jax.ShapeDtypeStruct((4, 4, PANEL[t], 128), bf16) for t, _ in order],
        scratch_shapes=[pltpu.SemaphoreType.DMA((84,))],
        compiler_params=params(),
        cost_estimate=cost(17_000_000),
    )(pos, *flat(got1, 0), *[got2[t][k] for t, k in ISSUE[1]])
    bufs = [[None] * 4 for _ in range(3)]
    for (t, k), o in zip(order, outs):
        bufs[t][k] = o
    return bufs


def panel_kernel(pos_ref, *refs):
    got = unflat(refs[:12], 2)
    s_ref, old_ref, pick_ref = refs[12:15]
    back = refs[15:27]
    sk_ref, sums_ref, diag_ref = refs[27:30]
    scr_in, scr_out = refs[30:33], refs[33:36]
    x_ref, s_vmem, acc_ref, skt_ref, sem, sem_s, sem_out = refs[36:]
    here = [pos_ref[i] for i in range(3)]

    loads = [
        pltpu.make_async_copy(got[t][k], scr_in[t].at[k], sem.at[4 * t + k]) for t in range(3) for k in range(4)
    ]
    loads.append(pltpu.make_async_copy(s_ref, s_vmem, sem_s))
    run_copies(loads)

    def lay(src, _):
        there = [src // 16, lax.rem(src // 4, 4), lax.rem(src, 4)]
        k = {a: lax.rem(there[i] + 4 - here[i], 4) for i, a in enumerate(AX)}
        row = pl.multiple_of(src * ROWS, 16)
        for t in range(3):
            o1, o2, o3 = ORDERS[t]
            block = scr_in[t].at[k[o3], k[o2], k[o1]]
            for l in range(NL):
                x_ref[pl.ds(row, ROWS), 512 * l + 128 * t : 512 * l + 128 * (t + 1)] = block[
                    ROWS * l : ROWS * (l + 1), :
                ]
            if t < 2:
                tail = block[160:176, :]
                for i in range(5):
                    x_ref[pl.ds(pl.multiple_of(row + 16 * i, 16), 16), 512 * t + 384 : 512 * t + 512] = (
                        jnp.concatenate([tail[:, 16 * i : 16 * i + 16], jnp.zeros((16, 112), bf16)], axis=1)
                    )
        return 0

    lax.fori_loop(0, N, lay, 0)

    acc_ref[...] = jnp.zeros_like(acc_ref)

    def add(i, _):
        rows = pl.ds(pl.multiple_of(i * 640, 640), 640)
        acc_ref[...] += lax.dot_general(
            s_vmem[rows, :], x_ref[rows, :], (((0,), (0,)), ((), ())), preferred_element_type=f32
        )
        return 0

    lax.fori_loop(0, 8, add, 0)
    for l in range(NL):
        wide = acc_ref[:, 512 * l : 512 * (l + 1)]
        skt = wide.astype(bf16)
        skt_ref[...] = skt
        sk = jnp.transpose(skt.astype(f32), (1, 0))
        diag_ref[l : l + 1, :] = jnp.sum(sk * sk, axis=0, keepdims=True)
        sk_ref[l] = sk.astype(bf16)
        chosen = jnp.dot(sk_ref[l], pick_ref[l], preferred_element_type=f32).astype(bf16)
        sums_ref[l, :, 0:RANK] = jnp.dot(skt_ref[...], chosen, preferred_element_type=f32).astype(bf16)
        sums_ref[l, :, RANK:KS] = jnp.dot(
            skt_ref[:, 0:COLS], old_ref[l], preferred_element_type=f32
        ).astype(bf16)

    def out(i, _):
        kz, kx = lax.rem(i // 4 + 4 - here[0], 4), lax.rem(lax.rem(i, 4) + 4 - here[1], 4)
        rows = pl.ds(pl.multiple_of(i * 4 * ROWS, 64), 4 * ROWS)
        for l in range(NL):
            part = jnp.dot(
                x_ref[rows, 512 * l : 512 * (l + 1)], sk_ref[l], preferred_element_type=f32
            ).astype(bf16)
            for y in range(4):
                ky = lax.rem(y + 4 - here[2], 4)
                one = part[ROWS * y : ROWS * (y + 1)]
                for t in range(3):
                    scr_out[t][kz, kx, ky, ROWS * l : ROWS * (l + 1), :] = one[:, 128 * t : 128 * (t + 1)]
                last = one[:, 384:512]
                if l == 0:
                    scr_out[0][kz, kx, ky, 160:208, :] = last[0:48]
                    scr_out[1][kz, kx, ky, 160:192, :] = last[48:80]
                else:
                    scr_out[1][kz, kx, ky, 192:208, :] = last[0:16]
                    scr_out[2][kz, kx, ky, 160:224, :] = last[16:80]
        return 0

    lax.fori_loop(0, 16, out, 0)
    stores = []
    for t in range(3):
        for k in range(4):
            src = scr_out[t]
            first = AX.index(ORDERS[t][0])
            src = (src.at[k], src.at[:, k], src.at[:, :, k])[first]
            stores.append(pltpu.make_async_copy(src, back[4 * t + k], sem_out.at[4 * t + k]))
    run_copies(stores)


def panel_products(pos, got, s, old, picker):
    outs = pl.pallas_call(
        panel_kernel,
        in_specs=[SMEM] + [HBM] * 13 + [INNER] * 2,
        out_specs=[HBM] * 12 + [INNER] * 3,
        out_shape=[jax.ShapeDtypeStruct((4, 4, n, 128), bf16) for n in BACK for _ in range(4)]
        + [
            jax.ShapeDtypeStruct((NL, KS, KS), bf16),
            jax.ShapeDtypeStruct((NL, KS, KS), bf16),
            jax.ShapeDtypeStruct((NL, KS), f32),
        ],
        scratch_shapes=[pltpu.VMEM((4, 4, 4, n, 128), bf16) for n in PANEL]
        + [pltpu.VMEM((4, 4, 4, n, 128), bf16) for n in BACK]
        + [
            pltpu.VMEM((N * ROWS, NL * 512), bf16),
            pltpu.VMEM((N * ROWS, KS), bf16),
            pltpu.VMEM((KS, NL * 512), f32),
            pltpu.VMEM((KS, 512), bf16),
            pltpu.SemaphoreType.DMA((12,)),
            pltpu.SemaphoreType.DMA,
            pltpu.SemaphoreType.DMA((12,)),
        ],
        compiler_params=params(),
        cost_estimate=cost(26_000_000, 11_000_000_000),
    )(pos, *flat(got, 2), s, old, picker)
    return [list(outs[4 * t : 4 * t + 4]) for t in range(3)], outs[12], outs[13], outs[14]


def reduce_kernel(stage, *refs):
    got = unflat(refs[:12], stage)
    outs = refs[12:]
    for t in range(3):
        axis = ORDERS[t][stage + 1]
        dim = rest_axes(t, stage + 1).index(axis)
        for k in range(4):
            out = outs[4 * t + k]
            if stage == 0:
                for i in range(4):
                    at = (k, i) if dim == 0 else (i, k)
                    out[i] = sum(got[t][j][at].astype(f32) for j in range(4)).astype(bf16)
            else:
                out[...] = sum(got[t][j][k].astype(f32) for j in range(4)).astype(bf16)


def reduce_stage(got, stage):
    lead = (4,) if stage == 0 else ()
    outs = pl.pallas_call(
        lambda *refs: reduce_kernel(stage, *refs),
        in_specs=[INNER] * 12,
        out_specs=[INNER] * 12,
        out_shape=[jax.ShapeDtypeStruct(lead + (n, 128), bf16) for n in BACK for _ in range(4)],
        compiler_params=params(),
        cost_estimate=cost(13_000_000 if stage == 0 else 3_300_000),
    )(*flat(got, stage))
    return [list(outs[4 * t : 4 * t + 4]) for t in range(3)]


def shift_back(bufs, stage):
    got = [[b[0], None, None, None] for b in bufs]
    for t, k in ISSUE[stage]:
        got[t][k] = shifted(bufs[t][4 - k], ORDERS[t][stage], k)
    return got


def shards(gradients, sketch, rank_lists, old_basis, first_moment, second_moment):
    full_sketch = lax.all_gather(sketch, AX, axis=0, tiled=True)
    pos = jnp.stack([lax.axis_index(a) for a in AX]).astype(jnp.int32)
    got1 = permute_stage(pack(pos, gradients), 0)
    got2 = permute_stage(second(pos, got1), 1)
    got3 = permute_stage(third(pos, got1, got2), 2)
    picker = (lax.broadcasted_iota(jnp.int32, (NL, KS, RANK), 1) == rank_lists[:, None, :]).astype(bf16)
    parts, sketched, sums, diag = panel_products(pos, got3, full_sketch, old_basis, picker)

    high = diag.astype(bf16)
    rest = diag - high.astype(f32)
    mid = rest.astype(bf16)
    low = (rest - mid.astype(f32)).astype(bf16)
    pieces = jnp.concatenate([high, mid, low, jnp.zeros((2, KS), bf16)], 0)
    blocks = sums.reshape(NL, N, 8, KS).transpose(1, 0, 2, 3).reshape(N, NL * 8, KS)
    send = jnp.concatenate([blocks, jnp.broadcast_to(pieces[None], (N, 8, KS))], 1)
    got = lax.all_to_all(send, AX, 0, 0, tiled=True)
    total = jnp.sum(got.astype(f32), axis=0)
    row_sums = total[: NL * 8].reshape(NL, 8, KS)
    diag = total[16:18] + total[18:20] + total[20:22]
    trace = jnp.sum(diag, axis=1)

    me = (lax.axis_index("z") * 4 + lax.axis_index("x")) * 4 + lax.axis_index("y")
    my_rows = me * 8 + lax.broadcasted_iota(jnp.int32, (8, RANK), 0)
    owned = []
    for l in range(NL):
        scale = 0.5 * KS / trace[l]
        rms = jnp.sqrt(trace[l] / (FF * KS))
        my_diag = lax.dynamic_slice_in_dim(diag[l], me * 8, 8, 0)[:, None]
        corrected = jnp.where(
            my_rows == rank_lists[l][None, :], 1.5 - scale * my_diag, -scale * row_sums[l][:, :RANK]
        )
        owned.append(
            jnp.concatenate([(corrected / rms).astype(bf16), row_sums[l][:, RANK:].astype(bf16)], 1)
        )
    mine = jnp.concatenate(owned, 0)
    everyone = lax.all_to_all(jnp.broadcast_to(mine[None], (N, NL * 8, KS)), AX, 0, 0, tiled=True)

    back = shift_back(parts, 0)
    back = shift_back(reduce_stage(back, 0), 1)
    back = shift_back(reduce_stage(back, 1), 2)
    t0, t1, t2 = [sum(p.astype(f32) for p in back[t]) for t in range(3)]
    last = (jnp.concatenate([t0[160:], t1[160:192]], 0), jnp.concatenate([t1[192:], t2[160:]], 0))

    basis_list, projected_list, first_list, second_list = [], [], [], []
    for l in range(NL):
        both = everyone[:, 8 * l : 8 * l + 8].reshape(KS, KS)
        factor, inner = both[:, :RANK], both[:, RANK:]
        basis_list.append(
            jnp.dot(sketched[l, :COLS], factor, preferred_element_type=f32).astype(bf16)
        )
        correlation = lax.dot_general(
            inner, factor, (((0,), (0,)), ((), ())), preferred_element_type=f32
        ) / math.sqrt(FF * RANK)
        rows = slice(ROWS * l, ROWS * (l + 1))
        t_rows = jnp.concatenate([t0[rows], t1[rows], t2[rows], last[l]], 1)
        projected_list.append(
            (jnp.dot(t_rows, factor.astype(f32), precision=highest) / math.sqrt(FF)).astype(bf16)
        )
        first_list.append(jnp.dot(first_moment[l], correlation, precision=highest))
        second_list.append(jnp.dot(second_moment[l], correlation * correlation, precision=highest))
    scores = lax.psum((diag[0] + diag[1]) / FF, "layer")
    return (
        jnp.stack(basis_list, 0),
        jnp.stack(projected_list, 0),
        jnp.stack(first_list, 0),
        jnp.stack(second_list, 0),
        scores,
    )


def solution(mesh):
    cube = Mesh(mesh.devices.reshape(4, 4, 4, 2), AX + ("layer",))
    rows = P("layer", AX, None)
    return jax.shard_map(
        shards,
        mesh=cube,
        in_specs=(rows, P(AX, None), P("layer", None), rows, rows, rows),
        out_specs=(rows, rows, rows, rows, P()),
        check_vma=False,
    )
```

```python
import math

import jax
import jax.numpy as jnp
from jax import lax
from jax.experimental import pallas as pl
from jax.experimental.pallas import tpu as pltpu
from jax.sharding import Mesh, PartitionSpec as P

FF = 25600
KS = 512
RANK = 256
ROWS = 80
COLS = 400
NL = 2
N = 64

bf16 = jnp.bfloat16
f32 = jnp.float32
highest = lax.Precision.HIGHEST
AX = ("z", "x", "y")
VMEM = 56 * 1024 * 1024

ORDERS = (("z", "x", "y"), ("x", "y", "z"), ("y", "z", "x"))
PANEL = (176, 176, 176)
BACK = (224, 224, 224)
ISSUE = ((0, 2), (1, 2), (2, 1), (2, 3), (0, 1), (0, 3), (1, 1), (1, 3), (2, 2))
HBM = pl.BlockSpec(memory_space=pl.ANY)
SMEM = pl.BlockSpec(memory_space=pltpu.SMEM)
INNER = pl.BlockSpec(memory_space=pltpu.VMEM)


def rest_axes(t, stage):
    return [a for a in AX if a in ORDERS[t][stage:]]


def shifted(x, axis, k):
    return lax.ppermute(x, axis, [(s, (s - k) % 4) for s in range(4)])


def params():
    return pltpu.CompilerParams(vmem_limit_bytes=VMEM)


def cost(nbytes, flops=0):
    return pl.CostEstimate(flops=flops, bytes_accessed=nbytes, transcendentals=0)


def run_copies(copies):
    for c in copies:
        c.start()
    for c in copies:
        c.wait()


def pass_on(loads, scr, outs, sem_out):
    for group in loads:
        for c in group:
            c.start()
    stores = []
    for at, group in enumerate(loads):
        for c in group:
            c.wait()
        stores.append(pltpu.make_async_copy(scr[at], outs[at], sem_out.at[at]))
        stores[-1].start()
    for c in stores:
        c.wait()


def pack_kernel(pos_ref, g_ref, *refs):
    outs, scr, sem = refs[:12], refs[12:15], refs[15]
    g = pl.program_id(0)
    here = [pos_ref[i] for i in range(3)]
    for j in range(8):
        there = [g // 2, 2 * lax.rem(g, 2) + j // 4, j % 4]
        tails = []
        for l in range(NL):
            rest = g_ref[l, :, COLS * j + 384 : COLS * (j + 1)]
            tails.append(
                jnp.concatenate(
                    [rest[16 * i : 16 * i + 16] for i in range(5)] + [jnp.zeros((16, 48), bf16)], axis=1
                )
            )
        for t in range(3):
            first = AX.index(ORDERS[t][0])
            other = [i for i in range(3) if i != first]
            k = lax.rem(here[first] - there[first] + 4, 4)
            at = there[other[0]] * 4 + there[other[1]]
            for l in range(NL):
                scr[t][k, at, pl.ds(ROWS * l, ROWS), :] = g_ref[
                    l, :, COLS * j + 128 * t : COLS * j + 128 * (t + 1)
                ]
            scr[t][k, at, pl.ds(160, 16), :] = tails[t] if t < 2 else jnp.zeros((16, 128), bf16)

    @pl.when(g == 7)
    def _():
        run_copies(
            [
                pltpu.make_async_copy(scr[t].at[k], outs[4 * t + k], sem.at[4 * t + k])
                for t in range(3)
                for k in range(4)
            ]
        )


def pack(pos, g):
    outs = pl.pallas_call(
        pack_kernel,
        grid=(8,),
        in_specs=[SMEM, pl.BlockSpec((NL, ROWS, 8 * COLS), lambda i: (0, 0, i))],
        out_specs=[HBM] * 12,
        out_shape=[jax.ShapeDtypeStruct((16, n, 128), bf16) for n in PANEL for _ in range(4)],
        scratch_shapes=[pltpu.VMEM((4, 16, n, 128), bf16) for n in PANEL] + [pltpu.SemaphoreType.DMA((12,))],
        compiler_params=params(),
        cost_estimate=cost(17_000_000),
    )(pos, g)
    return [[o.reshape((4, 4) + o.shape[1:]) for o in outs[4 * t : 4 * t + 4]] for t in range(3)]


def permute_stage(bufs, stage):
    got = [[b[0], None, None, None] for b in bufs]
    for t, k in ISSUE:
        got[t][k] = shifted(bufs[t][k], ORDERS[t][stage], k)
    return got


def flat(got, stage):
    return [got[t][k] for t, k in ISSUE] + [got[t][0] for t in range(3)]


def unflat(refs, stage):
    got = [[None] * 4 for _ in range(3)]
    for (t, k), r in zip(ISSUE, refs[:9]):
        got[t][k] = r
    for t in range(3):
        got[t][0] = refs[9 + t]
    return got


def second_kernel(pos_ref, *refs):
    first = unflat(refs[:12], 0)
    outs, scr, sem, sem_out = refs[12:21], refs[21:30], refs[30], refs[31]
    here = [pos_ref[i] for i in range(3)]
    loads = [[] for _ in outs]
    for at, (t, k) in enumerate(ISSUE):
        axis = ORDERS[t][1]
        place = lax.rem(here[AX.index(axis)] + 4 - k, 4)
        for k1 in range(4):
            src = first[t][k1]
            src = src.at[place] if rest_axes(t, 1).index(axis) == 0 else src.at[:, place]
            loads[at].append(pltpu.make_async_copy(src, scr[at].at[k1], sem.at[4 * at + k1]))
    pass_on(loads, scr, outs, sem_out)


def second(pos, got):
    outs = pl.pallas_call(
        second_kernel,
        in_specs=[SMEM] + [HBM] * 12,
        out_specs=[HBM] * 9,
        out_shape=[jax.ShapeDtypeStruct((4, 4, PANEL[t], 128), bf16) for t, _ in ISSUE],
        scratch_shapes=[pltpu.VMEM((4, 4, PANEL[t], 128), bf16) for t, _ in ISSUE]
        + [pltpu.SemaphoreType.DMA((36,)), pltpu.SemaphoreType.DMA((9,))],
        compiler_params=params(),
        cost_estimate=cost(13_000_000),
    )(pos, *flat(got, 0))
    bufs = [[None] * 4 for _ in range(3)]
    for (t, k), o in zip(ISSUE, outs):
        bufs[t][k] = o
    return bufs


def third_kernel(pos_ref, *refs):
    first = unflat(refs[:12], 0)
    later = [[None] * 4 for _ in range(3)]
    for (t, k), r in zip(ISSUE, refs[12:21]):
        later[t][k] = r
    outs, scr, sem, sem_out = refs[21:33], refs[33:45], refs[45], refs[46]
    here = [pos_ref[i] for i in range(3)]
    loads = [[] for _ in outs]
    for at, (t, k) in enumerate(ISSUE + ((0, 0), (1, 0), (2, 0))):
        axis2, axis3 = ORDERS[t][1], ORDERS[t][2]
        own = here[AX.index(axis2)]
        place = lax.rem(here[AX.index(axis3)] + 4 - k, 4)
        for k1 in range(4):
            src = first[t][k1]
            src = src.at[own, place] if rest_axes(t, 1).index(axis2) == 0 else src.at[place, own]
            loads[at].append(pltpu.make_async_copy(src, scr[at].at[0, k1], sem.at[7 * at + k1]))
        for k2 in range(1, 4):
            loads[at].append(
                pltpu.make_async_copy(later[t][k2].at[:, place], scr[at].at[k2], sem.at[7 * at + 3 + k2])
            )
    pass_on(loads, scr, outs, sem_out)


def third(pos, got1, got2):
    order = ISSUE + ((0, 0), (1, 0), (2, 0))
    outs = pl.pallas_call(
        third_kernel,
        in_specs=[SMEM] + [HBM] * 21,
        out_specs=[HBM] * 12,
        out_shape=[jax.ShapeDtypeStruct((4, 4, PANEL[t], 128), bf16) for t, _ in order],
        scratch_shapes=[pltpu.VMEM((4, 4, PANEL[t], 128), bf16) for t, _ in order]
        + [pltpu.SemaphoreType.DMA((84,)), pltpu.SemaphoreType.DMA((12,))],
        compiler_params=params(),
        cost_estimate=cost(17_000_000),
    )(pos, *flat(got1, 0), *[got2[t][k] for t, k in ISSUE])
    bufs = [[None] * 4 for _ in range(3)]
    for (t, k), o in zip(order, outs):
        bufs[t][k] = o
    return bufs


def panel_kernel(pos_ref, *refs):
    got = unflat(refs[:12], 2)
    s_ref, old_ref, pick_ref = refs[12:15]
    back = refs[15:27]
    sk_ref, send_ref = refs[27:29]
    scr_in, scr_out = refs[29:32], refs[32:35]
    x_ref, s_vmem, acc_ref, sem, sem_s, sem_out = refs[35:]
    here = [pos_ref[i] for i in range(3)]

    loads = [
        [pltpu.make_async_copy(got[t][k], scr_in[t].at[k], sem.at[4 * t + k]) for k in range(4)] for t in range(3)
    ]
    load_s = pltpu.make_async_copy(s_ref, s_vmem, sem_s)
    for c in loads[0] + loads[1] + loads[2] + [load_s]:
        c.start()
    acc_ref[...] = jnp.zeros_like(acc_ref)

    for t in range(3):
        for c in loads[t]:
            c.wait()

        def lay(src, _):
            there = [src // 16, lax.rem(src // 4, 4), lax.rem(src, 4)]
            k = {a: lax.rem(there[i] + 4 - here[i], 4) for i, a in enumerate(AX)}
            row = pl.multiple_of(src * ROWS, 16)
            o1, o2, o3 = ORDERS[t]
            block = scr_in[t].at[k[o3], k[o2], k[o1]]
            for l in range(NL):
                x_ref[pl.ds(row, ROWS), 512 * l + 128 * t : 512 * l + 128 * (t + 1)] = block[
                    ROWS * l : ROWS * (l + 1), :
                ]
            if t < 2:
                tail = block[160:176, :].astype(f32)
                for i in range(5):
                    turned = tail if i == 0 else pltpu.roll(tail, 128 - 16 * i, 1)
                    x_ref[pl.ds(pl.multiple_of(row + 16 * i, 16), 16), 512 * t + 384 : 512 * t + 512] = (
                        turned.astype(bf16)
                    )
            return 0

        lax.fori_loop(0, N, lay, 0)
    load_s.wait()

    def add(i, _):
        rows = pl.ds(pl.multiple_of(i * 640, 640), 640)
        acc_ref[...] += lax.dot_general(
            s_vmem[rows, :], x_ref[rows, :], (((0,), (0,)), ((), ())), preferred_element_type=f32
        )
        return 0

    lax.fori_loop(0, 8, add, 0)
    inside = lax.broadcasted_iota(jnp.int32, (KS, 512), 1) < COLS
    sums, pieces = [], []
    for l in range(NL):
        wide = jnp.where(inside, acc_ref[:, 512 * l : 512 * (l + 1)], 0.0)
        skt = wide.astype(bf16)
        sk = jnp.transpose(skt.astype(f32), (1, 0))
        diag = jnp.sum(sk * sk, axis=0, keepdims=True)
        high = diag.astype(bf16).astype(f32)
        for d in (high, diag - high):
            pieces += [d[:, 128 * i : 128 * (i + 1)] for i in range(4)]
        sk_ref[l] = sk.astype(bf16)
        chosen = jnp.dot(sk_ref[l], pick_ref[l], preferred_element_type=f32).astype(bf16)
        left = jnp.dot(skt, chosen, preferred_element_type=f32)
        right = jnp.dot(skt[:, 0:COLS], old_ref[l], preferred_element_type=f32)
        sums.append(jnp.concatenate([left, right], 1).reshape(N, 8, KS))
    send_ref[:, :, 0:KS] = jnp.concatenate(sums, 1).astype(bf16)
    send_ref[:, :, KS : KS + 128] = jnp.broadcast_to(
        jnp.concatenate(pieces, 0).astype(bf16)[None], (N, 16, 128)
    )

    stores = []

    def store(t, k):
        src = scr_out[t]
        src = (src.at[k], src.at[:, k], src.at[:, :, k])[AX.index(ORDERS[t][0])]
        stores.append(pltpu.make_async_copy(src, back[4 * t + k], sem_out.at[4 * t + k]))
        stores[-1].start()

    for kz in range(4):
        z = lax.rem(here[0] + kz, 4)

        def out(kx, _):
            x = lax.rem(here[1] + kx, 4)
            rows = pl.ds(pl.multiple_of((4 * z + x) * 4 * ROWS, 64), 4 * ROWS)
            for l in range(NL):
                part = jnp.dot(
                    x_ref[rows, 512 * l : 512 * (l + 1)], sk_ref[l], preferred_element_type=f32
                ).astype(bf16)
                for y in range(4):
                    ky = lax.rem(y + 4 - here[2], 4)
                    one = part[ROWS * y : ROWS * (y + 1)]
                    for t in range(3):
                        scr_out[t][kz, kx, ky, ROWS * l : ROWS * (l + 1), :] = one[:, 128 * t : 128 * (t + 1)]
                    last = one[:, 384:512]
                    if l == 0:
                        scr_out[0][kz, kx, ky, 160:208, :] = last[0:48]
                        scr_out[1][kz, kx, ky, 160:192, :] = last[48:80]
                    else:
                        scr_out[1][kz, kx, ky, 192:208, :] = last[0:16]
                        scr_out[2][kz, kx, ky, 160:224, :] = last[16:80]
            return 0

        lax.fori_loop(0, 4, out, 0)
        store(0, kz)
    for t in (1, 2):
        for k in range(4):
            store(t, k)
    for c in stores:
        c.wait()


def panel_products(pos, got, s, old, picker):
    outs = pl.pallas_call(
        panel_kernel,
        in_specs=[SMEM] + [HBM] * 13 + [INNER] * 2,
        out_specs=[HBM] * 12 + [INNER] * 2,
        out_shape=[jax.ShapeDtypeStruct((4, 4, n, 128), bf16) for n in BACK for _ in range(4)]
        + [jax.ShapeDtypeStruct((NL, KS, KS), bf16), jax.ShapeDtypeStruct((N, 16, KS + 128), bf16)],
        scratch_shapes=[pltpu.VMEM((4, 4, 4, n, 128), bf16) for n in PANEL]
        + [pltpu.VMEM((4, 4, 4, n, 128), bf16) for n in BACK]
        + [
            pltpu.VMEM((N * ROWS, NL * 512), bf16),
            pltpu.VMEM((N * ROWS, KS), bf16),
            pltpu.VMEM((KS, NL * 512), f32),
            pltpu.SemaphoreType.DMA((12,)),
            pltpu.SemaphoreType.DMA,
            pltpu.SemaphoreType.DMA((12,)),
        ],
        compiler_params=params(),
        cost_estimate=cost(26_000_000, 11_000_000_000),
    )(pos, *flat(got, 2), s, old, picker)
    return [list(outs[4 * t : 4 * t + 4]) for t in range(3)], outs[12], outs[13]


def owner_kernel(me_ref, got_ref, ranks_ref, mine_ref, scores_ref):
    total = jnp.sum(got_ref[...].astype(f32), axis=0)
    row = me_ref[0] * 8 + lax.broadcasted_iota(jnp.int32, (8, 128), 0)
    lane = lax.broadcasted_iota(jnp.int32, (8, 128), 1)
    my_rows = me_ref[0] * 8 + lax.broadcasted_iota(jnp.int32, (8, RANK), 0)
    owned, scores = [], 0.0
    for l in range(NL):
        diag = total[8 * l : 8 * l + 4, KS:] + total[8 * l + 4 : 8 * l + 8, KS:]
        scores = scores + diag
        trace = jnp.sum(jnp.sum(diag, axis=1, keepdims=True), axis=0, keepdims=True)
        mine = jnp.zeros((8, 128), f32)
        for c in range(4):
            mine = mine + jnp.where(lane + 128 * c == row, diag[c : c + 1, :], 0.0)
        my_diag = jnp.sum(mine, axis=1, keepdims=True)
        scale = 0.5 * KS / trace
        rms = jnp.sqrt(trace / (FF * KS))
        gram = total[8 * l : 8 * l + 8, 0:RANK]
        corrected = jnp.where(my_rows == ranks_ref[l : l + 1, :], 1.5 - scale * my_diag, -scale * gram)
        owned.append(jnp.concatenate([corrected / rms, total[8 * l : 8 * l + 8, RANK:KS]], 1))
    mine_ref[...] = jnp.broadcast_to(jnp.concatenate(owned, 0).astype(bf16)[None], (N, 16, KS))
    scores_ref[...] = scores / FF


def owner_rows(me, got, ranks):
    return pl.pallas_call(
        owner_kernel,
        in_specs=[SMEM, INNER, INNER],
        out_specs=[INNER, INNER],
        out_shape=[jax.ShapeDtypeStruct((N, 16, KS), bf16), jax.ShapeDtypeStruct((4, 128), f32)],
        compiler_params=params(),
        cost_estimate=cost(2_500_000),
    )(me, got, ranks)


def moments_kernel(rows_ref, sk_ref, one_ref, two_ref, basis_ref, first_ref, second_ref, factor_ref):
    rows = rows_ref[...].astype(f32)
    for l in range(NL):
        both = rows[:, 8 * l : 8 * l + 8, :].reshape(KS, KS).astype(bf16)
        factor, inner = both[:, :RANK], both[:, RANK:]
        factor_ref[l] = factor
        basis_ref[l] = jnp.dot(sk_ref[l, 0:COLS, :], factor, preferred_element_type=f32).astype(bf16)
        correlation = lax.dot_general(
            inner, factor, (((0,), (0,)), ((), ())), preferred_element_type=f32
        ) / math.sqrt(FF * RANK)
        first_ref[l] = jnp.dot(one_ref[l], correlation, precision=highest, preferred_element_type=f32)
        second_ref[l] = jnp.dot(
            two_ref[l], correlation * correlation, precision=highest, preferred_element_type=f32
        )


def moments(rows, sk, one, two):
    return pl.pallas_call(
        moments_kernel,
        in_specs=[INNER] * 4,
        out_specs=[INNER] * 4,
        out_shape=[
            jax.ShapeDtypeStruct((NL, COLS, RANK), bf16),
            jax.ShapeDtypeStruct((NL, ROWS, RANK), f32),
            jax.ShapeDtypeStruct((NL, ROWS, RANK), f32),
            jax.ShapeDtypeStruct((NL, KS, RANK), bf16),
        ],
        compiler_params=params(),
        cost_estimate=cost(4_000_000, 500_000_000),
    )(rows, sk, one, two)


def project_kernel(*refs):
    got = unflat(refs[:12], 2)
    factor_ref, out_ref = refs[12:]
    t0, t1, t2 = [sum(got[t][k][...].astype(f32) for k in range(4)) for t in range(3)]
    last = (jnp.concatenate([t0[160:208], t1[160:192]], 0), jnp.concatenate([t1[192:208], t2[160:224]], 0))
    for l in range(NL):
        rows = slice(ROWS * l, ROWS * (l + 1))
        t_rows = jnp.concatenate([t0[rows], t1[rows], t2[rows], last[l]], 1)
        out_ref[l] = (
            jnp.dot(t_rows, factor_ref[l].astype(f32), precision=highest, preferred_element_type=f32)
            / math.sqrt(FF)
        ).astype(bf16)


def project(got, factor):
    return pl.pallas_call(
        project_kernel,
        in_specs=[INNER] * 13,
        out_specs=INNER,
        out_shape=jax.ShapeDtypeStruct((NL, ROWS, RANK), bf16),
        compiler_params=params(),
        cost_estimate=cost(2_000_000, 100_000_000),
    )(*flat(got, 2), factor)


def reduce_kernel(stage, *refs):
    got = unflat(refs[:12], stage)
    outs = refs[12:]
    for t in range(3):
        axis = ORDERS[t][stage + 1]
        dim = rest_axes(t, stage + 1).index(axis)
        for k in range(4):
            out = outs[4 * t + k]
            if stage == 0:
                for i in range(4):
                    at = (k, i) if dim == 0 else (i, k)
                    out[i] = sum(got[t][j][at].astype(f32) for j in range(4)).astype(bf16)
            else:
                out[...] = sum(got[t][j][k].astype(f32) for j in range(4)).astype(bf16)


def reduce_stage(got, stage):
    lead = (4,) if stage == 0 else ()
    outs = pl.pallas_call(
        lambda *refs: reduce_kernel(stage, *refs),
        in_specs=[INNER] * 12,
        out_specs=[INNER] * 12,
        out_shape=[jax.ShapeDtypeStruct(lead + (n, 128), bf16) for n in BACK for _ in range(4)],
        compiler_params=params(),
        cost_estimate=cost(13_000_000 if stage == 0 else 3_300_000),
    )(*flat(got, stage))
    return [list(outs[4 * t : 4 * t + 4]) for t in range(3)]


def shift_back(bufs, stage):
    got = [[b[0], None, None, None] for b in bufs]
    for t, k in ISSUE:
        got[t][k] = shifted(bufs[t][4 - k], ORDERS[t][stage], k)
    return got


def shards(gradients, sketch, rank_lists, old_basis, first_moment, second_moment):
    full_sketch = lax.all_gather(sketch, AX, axis=0, tiled=True)
    pos = jnp.stack([lax.axis_index(a) for a in AX]).astype(jnp.int32)
    got1 = permute_stage(pack(pos, gradients), 0)
    got2 = permute_stage(second(pos, got1), 1)
    got3 = permute_stage(third(pos, got1, got2), 2)
    picker = (lax.broadcasted_iota(jnp.int32, (NL, KS, RANK), 1) == rank_lists[:, None, :]).astype(bf16)
    parts, sketched, send = panel_products(pos, got3, full_sketch, old_basis, picker)
    got = lax.all_to_all(send, AX, 0, 0, tiled=True)
    me = (16 * pos[0] + 4 * pos[1] + pos[2])[None]
    mine, scores = owner_rows(me, got, rank_lists)
    everyone = lax.all_to_all(mine, AX, 0, 0, tiled=True)
    basis, first, second_out, factor = moments(everyone, sketched, first_moment, second_moment)
    back = shift_back(parts, 0)
    back = shift_back(reduce_stage(back, 0), 1)
    back = shift_back(reduce_stage(back, 1), 2)
    projected = project(back, factor)
    return basis, projected, first, second_out, lax.psum(scores.reshape(KS), "layer")


def solution(mesh):
    cube = Mesh(mesh.devices.reshape(4, 4, 4, 2), AX + ("layer",))
    rows = P("layer", AX, None)
    return jax.shard_map(
        shards,
        mesh=cube,
        in_specs=(rows, P(AX, None), P("layer", None), rows, rows, rows),
        out_specs=(rows, rows, rows, rows, P()),
        check_vma=False,
    )
```

```python
import math

import jax
import jax.numpy as jnp
from jax import lax
from jax.experimental import pallas as pl
from jax.experimental.pallas import tpu as pltpu
from jax.sharding import Mesh, PartitionSpec as P

FF = 25600
KS = 512
RANK = 256
ROWS = 80
COLS = 400
NL = 2
N = 64
WIDE = 4 * COLS
LANES = 1664

bf16 = jnp.bfloat16
f32 = jnp.float32
highest = lax.Precision.HIGHEST
AX = ("z", "x", "y")
VMEM = 56 * 1024 * 1024

ORDERS = (("z", "x", "y"), ("y", "z", "x"))
ISSUE = ((1, 1), (1, 3), (0, 1), (0, 3), (0, 2), (1, 2))
HBM = pl.BlockSpec(memory_space=pl.ANY)
SMEM = pl.BlockSpec(memory_space=pltpu.SMEM)
INNER = pl.BlockSpec(memory_space=pltpu.VMEM)


def shifted(x, axis, k):
    return lax.ppermute(x, axis, [(s, (s - k) % 4) for s in range(4)])


def params():
    return pltpu.CompilerParams(vmem_limit_bytes=VMEM)


def cost(nbytes, flops=0):
    return pl.CostEstimate(flops=flops, bytes_accessed=nbytes, transcendentals=0)


def pack_kernel(pos_ref, g_ref, *refs):
    outs, scr, sem = refs[:8], refs[8:10], refs[10]
    z = pl.program_id(0)
    kz = lax.rem(pos_ref[0] - z + 4, 4)

    def put(block, strips):
        wide = jnp.concatenate(strips + [jnp.zeros((ROWS, LANES - WIDE), bf16)], axis=1)
        block[...] = wide

    for i in range(4):
        put(scr[0].at[kz, i], [g_ref[0, :, WIDE * i : WIDE * (i + 1)]])
        ky = lax.rem(pos_ref[2] - i + 4, 4)
        put(
            scr[1].at[ky, z],
            [g_ref[1, :, WIDE * x + COLS * i : WIDE * x + COLS * (i + 1)] for x in range(4)],
        )
    for k in range(4):

        @pl.when(kz == k)
        def _():
            pltpu.make_async_copy(scr[0].at[k], outs[k], sem.at[k]).start()

        pltpu.make_async_copy(scr[1].at[k, z], outs[4 + k].at[z], sem.at[4 + k]).start()

    @pl.when(z == 3)
    def _():
        for l in range(NL):
            for k in range(4):
                pltpu.make_async_copy(scr[l].at[k], outs[4 * l + k], sem.at[4 * l + k]).wait()


def pack(pos, g):
    outs = pl.pallas_call(
        pack_kernel,
        grid=(4,),
        in_specs=[SMEM, pl.BlockSpec((NL, ROWS, 4 * WIDE), lambda i: (0, 0, i))],
        out_specs=[HBM] * 8,
        out_shape=[jax.ShapeDtypeStruct((4, ROWS, LANES), bf16)] * 8,
        scratch_shapes=[pltpu.VMEM((4, 4, ROWS, LANES), bf16)] * 2 + [pltpu.SemaphoreType.DMA((8,))],
        compiler_params=params(),
        cost_estimate=cost(17_000_000),
    )(pos, g)
    return [list(outs[:4]), list(outs[4:])]


def permute_stage(bufs, stage):
    got = [[b[0], None, None, None] for b in bufs]
    for l, k in ISSUE:
        got[l][k] = shifted(bufs[l][k], ORDERS[l][stage], k)
    return got


def moved(got):
    return [got[l][k] for l, k in ISSUE]


def flat(got):
    return moved(got) + [got[l][0] for l in range(NL)]


def unflat(refs):
    got = [[None] * 4 for _ in range(NL)]
    for (l, k), r in zip(ISSUE, refs):
        got[l][k] = r
    for l, r in enumerate(refs[6:]):
        got[l][0] = r
    return got


def second_kernel(pos_ref, *refs):
    first = unflat(refs[:8])
    outs, scr, sem, sem_out = refs[8:14], refs[14:20], refs[20], refs[21]
    loads = [[] for _ in outs]
    for at, (l, k) in enumerate(ISSUE):
        place = lax.rem(pos_ref[AX.index(ORDERS[l][1])] + 4 - k, 4)
        for k1 in range(4):
            loads[at].append(
                pltpu.make_async_copy(first[l][k1].at[place], scr[at].at[k1], sem.at[4 * at + k1])
            )
    for group in loads:
        for c in group:
            c.start()
    stores = []
    for at, group in enumerate(loads):
        for c in group:
            c.wait()
        stores.append(pltpu.make_async_copy(scr[at], outs[at], sem_out.at[at]))
        stores[-1].start()
    for c in stores:
        c.wait()


def second(pos, got):
    outs = pl.pallas_call(
        second_kernel,
        in_specs=[SMEM] + [HBM] * 8,
        out_specs=[HBM] * 6,
        out_shape=[jax.ShapeDtypeStruct((4, ROWS, LANES), bf16)] * 6,
        scratch_shapes=[pltpu.VMEM((4, ROWS, LANES), bf16)] * 6
        + [pltpu.SemaphoreType.DMA((24,)), pltpu.SemaphoreType.DMA((6,))],
        compiler_params=params(),
        cost_estimate=cost(13_000_000),
    )(pos, *flat(got))
    bufs = [[None] * 4 for _ in range(NL)]
    for (l, k), o in zip(ISSUE, outs):
        bufs[l][k] = o
    return bufs


def panel_loads(pos_ref, first, got, x_ref, sem):
    loads = []
    for l in range(NL):
        own = pos_ref[AX.index(ORDERS[l][1])]
        copies = []
        for k in range(4):
            dst = x_ref.at[l, k, 0] if l == 0 else x_ref.at[l, 0, k]
            copies.append(pltpu.make_async_copy(first[l][k].at[own], dst, sem.at[8 * l + k]))
            if k:
                dst = x_ref.at[l, :, k] if l == 0 else x_ref.at[l, k]
                copies.append(pltpu.make_async_copy(got[l][k], dst, sem.at[8 * l + 4 + k]))
        for c in copies:
            c.start()
        loads.append(copies)
    return loads


def panel_kernel(pos_ref, *refs):
    first, got = unflat(refs[:8]), unflat(refs[8:14])
    s_ref = refs[14:16]
    outs = refs[16:24]
    x_ref, s_vmem, acc_ref, u_ref, sem, sem_s, sem_out = refs[24:]
    load_s = []
    for l in range(NL):
        for kz in range(4):
            for k in range(4):
                z, other = lax.rem(pos_ref[0] + kz, 4), lax.rem(pos_ref[1 + l] + k, 4)
                at = 16 * l + 4 * kz + k
                load_s.append(
                    pltpu.make_async_copy(s_ref[l].at[4 * z + other], s_vmem.at[l, kz, k], sem_s.at[at])
                )
                load_s[-1].start()
    loads = panel_loads(pos_ref, first, got, x_ref, sem)
    for c in load_s:
        c.wait()
    stores = []
    for l in range(NL):
        for c in loads[l]:
            c.wait()
        for i in range(2):
            part = lax.dot_general(
                s_vmem[l, 2 * i : 2 * i + 2].reshape(8 * ROWS, KS),
                x_ref[l, 2 * i : 2 * i + 2].reshape(8 * ROWS, LANES),
                (((0,), (0,)), ((), ())),
                preferred_element_type=f32,
            )
            acc_ref[...] = part if i == 0 else acc_ref[...] + part
        u_ref[l] = jnp.transpose(acc_ref[...], (1, 0)).astype(bf16)
        stores += [
            pltpu.make_async_copy(u_ref.at[l, rows], outs[4 * l + k], sem_out.at[4 * l + k])
            for k, rows in strips(pos_ref, l)
        ]
        for c in stores[-4:]:
            c.start()
    for c in stores:
        c.wait()


def strips(pos_ref, l):
    me = pos_ref[AX.index(ORDERS[l][2])]
    return [(k, pl.ds(pl.multiple_of(lax.rem(me + k, 4) * COLS, 16), COLS)) for k in range(4)]


def panel_products(pos, got1, got2, s):
    outs = pl.pallas_call(
        panel_kernel,
        in_specs=[SMEM] + [HBM] * 16,
        out_specs=[HBM] * 8,
        out_shape=[jax.ShapeDtypeStruct((COLS, KS), bf16)] * 8,
        scratch_shapes=[
            pltpu.VMEM((NL, 4, 4, ROWS, LANES), bf16),
            pltpu.VMEM((NL, 4, 4, ROWS, KS), bf16),
            pltpu.VMEM((KS, LANES), f32),
            pltpu.VMEM((NL, LANES, KS), bf16),
            pltpu.SemaphoreType.DMA((16,)),
            pltpu.SemaphoreType.DMA((32,)),
            pltpu.SemaphoreType.DMA((8,)),
        ],
        compiler_params=params(),
        cost_estimate=cost(15_000_000, 4_400_000_000),
    )(pos, *flat(got1), *moved(got2), *s)
    return [list(outs[:4]), list(outs[4:])]


def gram_kernel(*refs):
    got = unflat(refs[:8])
    old_ref, pick_ref = refs[8:10]
    sk_refs, send_ref = refs[10:12], refs[12]
    sums, pieces = [], []
    for l in range(NL):
        parts = [r[...].astype(f32) for r in got[l]]
        sk = (parts[0] + parts[1] + parts[2] + parts[3]).astype(bf16)
        sk_refs[l][...] = sk
        wide = sk.astype(f32)
        diag = jnp.sum(wide * wide, axis=0, keepdims=True)
        high = diag.astype(bf16).astype(f32)
        for d in (high, diag - high):
            pieces += [d[:, 128 * i : 128 * (i + 1)] for i in range(4)]
        chosen = jnp.dot(sk, pick_ref[l], preferred_element_type=f32).astype(bf16)
        right = jnp.concatenate([chosen, old_ref[l]], 1)
        both = lax.dot_general(sk, right, (((0,), (0,)), ((), ())), preferred_element_type=f32)
        sums.append(both.reshape(N, 8, KS))
    send_ref[:, :, 0:KS] = jnp.concatenate(sums, 1).astype(bf16)
    send_ref[:, :, KS : KS + 128] = jnp.broadcast_to(
        jnp.concatenate(pieces, 0).astype(bf16)[None], (N, 16, 128)
    )


def gram_products(got, old, picker):
    outs = pl.pallas_call(
        gram_kernel,
        in_specs=[INNER] * 10,
        out_specs=[INNER] * 3,
        out_shape=[jax.ShapeDtypeStruct((COLS, KS), bf16)] * 2
        + [jax.ShapeDtypeStruct((N, 16, KS + 128), bf16)],
        compiler_params=params(),
        cost_estimate=cost(7_000_000, 1_000_000_000),
    )(*flat(got), old, picker)
    return list(outs[:2]), outs[2]


def back_kernel(pos_ref, *refs):
    first, got = unflat(refs[:8]), unflat(refs[8:14])
    sk_in = unflat(refs[14:22])
    outs = refs[22:30]
    x_ref, sk_ref, t_ref, sem, sem_s, sem_out = refs[30:]
    load_s = []
    for l in range(NL):
        for k, rows in strips(pos_ref, l):
            load_s.append(pltpu.make_async_copy(sk_in[l][k], sk_ref.at[l, rows], sem_s.at[4 * l + k]))
            load_s[-1].start()
    loads = panel_loads(pos_ref, first, got, x_ref, sem)
    for l in range(NL):
        sk_ref[l, WIDE:LANES, :] = jnp.zeros((LANES - WIDE, KS), bf16)
    for c in load_s:
        c.wait()
    stores = []
    for l in range(NL):
        for c in loads[l]:
            c.wait()
        for kz in range(4):
            t_ref[l, kz] = (
                jnp.dot(x_ref[l, kz].reshape(4 * ROWS, LANES), sk_ref[l], preferred_element_type=f32)
                .astype(bf16)
                .reshape(4, ROWS, KS)
            )
            if l == 0:
                stores.append(pltpu.make_async_copy(t_ref.at[0, kz], outs[kz], sem_out.at[kz]))
                stores[-1].start()
                continue
            for k in range(4):
                stores.append(
                    pltpu.make_async_copy(t_ref.at[1, kz, k], outs[4 + k].at[kz], sem_out.at[4 + 4 * kz + k])
                )
                stores[-1].start()
    for c in stores:
        c.wait()


def back_products(pos, got1, got2, sks):
    outs = pl.pallas_call(
        back_kernel,
        in_specs=[SMEM] + [HBM] * 22,
        out_specs=[HBM] * 8,
        out_shape=[jax.ShapeDtypeStruct((4, ROWS, KS), bf16)] * 8,
        scratch_shapes=[
            pltpu.VMEM((NL, 4, 4, ROWS, LANES), bf16),
            pltpu.VMEM((NL, LANES, KS), bf16),
            pltpu.VMEM((NL, 4, 4, ROWS, KS), bf16),
            pltpu.SemaphoreType.DMA((16,)),
            pltpu.SemaphoreType.DMA((8,)),
            pltpu.SemaphoreType.DMA((20,)),
        ],
        compiler_params=params(),
        cost_estimate=cost(16_000_000, 4_400_000_000),
    )(pos, *flat(got1), *moved(got2), *flat(sks))
    return [list(outs[:4]), list(outs[4:])]


def owner_kernel(me_ref, got_ref, ranks_ref, mine_ref, scores_ref):
    total = jnp.sum(got_ref[...].astype(f32), axis=0)
    row = me_ref[0] * 8 + lax.broadcasted_iota(jnp.int32, (8, 128), 0)
    lane = lax.broadcasted_iota(jnp.int32, (8, 128), 1)
    my_rows = me_ref[0] * 8 + lax.broadcasted_iota(jnp.int32, (8, RANK), 0)
    owned, scores = [], 0.0
    for l in range(NL):
        diag = total[8 * l : 8 * l + 4, KS:] + total[8 * l + 4 : 8 * l + 8, KS:]
        scores = scores + diag
        trace = jnp.sum(jnp.sum(diag, axis=1, keepdims=True), axis=0, keepdims=True)
        mine = jnp.zeros((8, 128), f32)
        for c in range(4):
            mine = mine + jnp.where(lane + 128 * c == row, diag[c : c + 1, :], 0.0)
        my_diag = jnp.sum(mine, axis=1, keepdims=True)
        scale = 0.5 * KS / trace
        rms = jnp.sqrt(trace / (FF * KS))
        gram = total[8 * l : 8 * l + 8, 0:RANK]
        corrected = jnp.where(my_rows == ranks_ref[l : l + 1, :], 1.5 - scale * my_diag, -scale * gram)
        owned.append(jnp.concatenate([corrected / rms, total[8 * l : 8 * l + 8, RANK:KS]], 1))
    mine_ref[...] = jnp.concatenate(owned, 0).astype(bf16)
    scores_ref[...] = scores / FF


def owner_rows(me, got, ranks):
    return pl.pallas_call(
        owner_kernel,
        in_specs=[SMEM, INNER, INNER],
        out_specs=[INNER, INNER],
        out_shape=[jax.ShapeDtypeStruct((16, KS), bf16), jax.ShapeDtypeStruct((4, 128), f32)],
        compiler_params=params(),
        cost_estimate=cost(2_500_000),
    )(me, got, ranks)


def moments_kernel(rows_ref, sk0_ref, sk1_ref, one_ref, two_ref, basis_ref, first_ref, second_ref, factor_ref):
    rows = rows_ref[...].astype(f32)
    for l in range(NL):
        both = rows[:, 8 * l : 8 * l + 8, :].reshape(KS, KS).astype(bf16)
        factor, inner = both[:, :RANK], both[:, RANK:]
        factor_ref[l] = factor
        sk = (sk0_ref, sk1_ref)[l][...]
        basis_ref[l] = jnp.dot(sk, factor, preferred_element_type=f32).astype(bf16)
        correlation = lax.dot_general(
            inner, factor, (((0,), (0,)), ((), ())), preferred_element_type=f32
        ) / math.sqrt(FF * RANK)
        first_ref[l] = jnp.dot(one_ref[l], correlation, precision=highest, preferred_element_type=f32)
        second_ref[l] = jnp.dot(
            two_ref[l], correlation * correlation, precision=highest, preferred_element_type=f32
        )


def moments(rows, sk, one, two):
    return pl.pallas_call(
        moments_kernel,
        in_specs=[INNER] * 5,
        out_specs=[INNER] * 4,
        out_shape=[
            jax.ShapeDtypeStruct((NL, COLS, RANK), bf16),
            jax.ShapeDtypeStruct((NL, ROWS, RANK), f32),
            jax.ShapeDtypeStruct((NL, ROWS, RANK), f32),
            jax.ShapeDtypeStruct((NL, KS, RANK), bf16),
        ],
        compiler_params=params(),
        cost_estimate=cost(4_000_000, 500_000_000),
    )(rows, *sk, one, two)


def project_kernel(*refs):
    got = unflat(refs[:8])
    factor_ref, out_ref = refs[8:]
    for l in range(NL):
        t_rows = sum(got[l][k][...].astype(f32) for k in range(4))
        out_ref[l] = (
            jnp.dot(t_rows, factor_ref[l].astype(f32), precision=highest, preferred_element_type=f32)
            / math.sqrt(FF)
        ).astype(bf16)


def project(got, factor):
    return pl.pallas_call(
        project_kernel,
        in_specs=[INNER] * 9,
        out_specs=INNER,
        out_shape=jax.ShapeDtypeStruct((NL, ROWS, RANK), bf16),
        compiler_params=params(),
        cost_estimate=cost(2_000_000, 100_000_000),
    )(*flat(got), factor)


def reduce_kernel(*refs):
    got = unflat(refs[:8])
    outs = refs[8:]
    for l in range(NL):
        for k in range(4):
            outs[4 * l + k][...] = sum(got[l][j][k].astype(f32) for j in range(4)).astype(bf16)


def reduce_stage(got):
    outs = pl.pallas_call(
        reduce_kernel,
        in_specs=[INNER] * 8,
        out_specs=[INNER] * 8,
        out_shape=[jax.ShapeDtypeStruct((ROWS, KS), bf16)] * 8,
        compiler_params=params(),
        cost_estimate=cost(3_300_000),
    )(*flat(got))
    return [list(outs[:4]), list(outs[4:])]


def shift_back(bufs, stage):
    got = [[b[0], None, None, None] for b in bufs]
    for l, k in ISSUE:
        got[l][k] = shifted(bufs[l][4 - k], ORDERS[l][stage], k)
    return got


def shards(gradients, sketch, rank_lists, old_basis, first_moment, second_moment):
    s_rows = [lax.all_gather(sketch, axes, axis=0) for axes in (("z", "x"), ("z", "y"))]
    pos = jnp.stack([lax.axis_index(a) for a in AX]).astype(jnp.int32)
    got1 = permute_stage(pack(pos, gradients), 0)
    got2 = permute_stage(second(pos, got1), 1)
    picker = (lax.broadcasted_iota(jnp.int32, (NL, KS, RANK), 1) == rank_lists[:, None, :]).astype(bf16)
    parts = shift_back(panel_products(pos, got1, got2, s_rows), 2)
    sketched, send = gram_products(parts, old_basis, picker)
    got = lax.all_to_all(send, AX, 0, 0, tiled=True)
    sks = permute_stage([[sk] * 4 for sk in sketched], 2)
    me = (16 * pos[0] + 4 * pos[1] + pos[2])[None]
    mine, scores = owner_rows(me, got, rank_lists)
    everyone = lax.all_gather(mine, AX, axis=0)
    basis, first, second_out, factor = moments(everyone, sketched, first_moment, second_moment)
    back = shift_back(back_products(pos, got1, got2, sks), 0)
    back = shift_back(reduce_stage(back), 1)
    projected = project(back, factor)
    scores = scores + lax.ppermute(scores, "layer", [(0, 1), (1, 0)])
    return basis, projected, first, second_out, scores.reshape(KS)


def solution(mesh):
    cube = Mesh(mesh.devices.reshape(4, 4, 4, 2), AX + ("layer",))
    rows = P("layer", AX, None)
    return jax.shard_map(
        shards,
        mesh=cube,
        in_specs=(rows, P(AX, None), P("layer", None), rows, rows, rows),
        out_specs=(rows, rows, rows, rows, P()),
        check_vma=False,
    )
```

```python
import math

import jax
import jax.numpy as jnp
from jax import lax
from jax.experimental import pallas as pl
from jax.experimental.pallas import tpu as pltpu
from jax.sharding import Mesh, PartitionSpec as P

FF = 25600
KS = 512
RANK = 256
ROWS = 80
COLS = 400
NL = 2
N = 64
WIDE = 4 * COLS
LANES = 1664

bf16 = jnp.bfloat16
f32 = jnp.float32
highest = lax.Precision.HIGHEST
AX = ("z", "x", "y")
VMEM = 56 * 1024 * 1024

ORDERS = (("z", "x", "y"), ("y", "z", "x"))
ISSUE = ((1, 1), (1, 3), (0, 1), (0, 3), (0, 2), (1, 2))
HBM = pl.BlockSpec(memory_space=pl.ANY)
SMEM = pl.BlockSpec(memory_space=pltpu.SMEM)
INNER = pl.BlockSpec(memory_space=pltpu.VMEM)


def shifted(x, axis, k):
    return lax.ppermute(x, axis, [(s, (s - k) % 4) for s in range(4)])


def params():
    return pltpu.CompilerParams(vmem_limit_bytes=VMEM)


def cost(nbytes, flops=0):
    return pl.CostEstimate(flops=flops, bytes_accessed=nbytes, transcendentals=0)


def pack_kernel(pos_ref, g_ref, *refs):
    outs, scr, sem = refs[:8], refs[8:10], refs[10]
    z = pl.program_id(0)
    kz = lax.rem(pos_ref[0] - z + 4, 4)

    def put(block, strips):
        wide = jnp.concatenate(strips + [jnp.zeros((ROWS, LANES - WIDE), bf16)], axis=1)
        block[...] = wide

    for i in range(4):
        put(scr[0].at[kz, i], [g_ref[0, :, WIDE * i : WIDE * (i + 1)]])
        ky = lax.rem(pos_ref[2] - i + 4, 4)
        put(
            scr[1].at[ky, z],
            [g_ref[1, :, WIDE * x + COLS * i : WIDE * x + COLS * (i + 1)] for x in range(4)],
        )
    for k in range(4):

        @pl.when(kz == k)
        def _():
            pltpu.make_async_copy(scr[0].at[k], outs[k], sem.at[k]).start()

        pltpu.make_async_copy(scr[1].at[k, z], outs[4 + k].at[z], sem.at[4 + k]).start()

    @pl.when(z == 3)
    def _():
        for l in range(NL):
            for k in range(4):
                pltpu.make_async_copy(scr[l].at[k], outs[4 * l + k], sem.at[4 * l + k]).wait()


def pack(pos, g):
    outs = pl.pallas_call(
        pack_kernel,
        grid=(4,),
        in_specs=[SMEM, pl.BlockSpec((NL, ROWS, 4 * WIDE), lambda i: (0, 0, i))],
        out_specs=[HBM] * 8,
        out_shape=[jax.ShapeDtypeStruct((4, ROWS, LANES), bf16)] * 8,
        scratch_shapes=[pltpu.VMEM((4, 4, ROWS, LANES), bf16)] * 2 + [pltpu.SemaphoreType.DMA((8,))],
        compiler_params=params(),
        cost_estimate=cost(17_000_000),
    )(pos, g)
    return [list(outs[:4]), list(outs[4:])]


def permute_stage(bufs, stage):
    got = [[b[0], None, None, None] for b in bufs]
    for l, k in ISSUE:
        got[l][k] = shifted(bufs[l][k], ORDERS[l][stage], k)
    return got


def moved(got):
    return [got[l][k] for l, k in ISSUE]


def flat(got):
    return moved(got) + [got[l][0] for l in range(NL)]


def unflat(refs):
    got = [[None] * 4 for _ in range(NL)]
    for (l, k), r in zip(ISSUE, refs):
        got[l][k] = r
    for l, r in enumerate(refs[6:]):
        got[l][0] = r
    return got


def second_kernel(pos_ref, *refs):
    first = unflat(refs[:8])
    outs, scr, sem, sem_out = refs[8:14], refs[14:20], refs[20], refs[21]
    loads = [[] for _ in outs]
    for at, (l, k) in enumerate(ISSUE):
        place = lax.rem(pos_ref[AX.index(ORDERS[l][1])] + 4 - k, 4)
        for k1 in range(4):
            loads[at].append(
                pltpu.make_async_copy(first[l][k1].at[place], scr[at].at[k1], sem.at[4 * at + k1])
            )
    for group in loads:
        for c in group:
            c.start()
    stores = []
    for at, group in enumerate(loads):
        for c in group:
            c.wait()
        stores.append(pltpu.make_async_copy(scr[at], outs[at], sem_out.at[at]))
        stores[-1].start()
    for c in stores:
        c.wait()


def second(pos, got):
    outs = pl.pallas_call(
        second_kernel,
        in_specs=[SMEM] + [HBM] * 8,
        out_specs=[HBM] * 6,
        out_shape=[jax.ShapeDtypeStruct((4, ROWS, LANES), bf16)] * 6,
        scratch_shapes=[pltpu.VMEM((4, ROWS, LANES), bf16)] * 6
        + [pltpu.SemaphoreType.DMA((24,)), pltpu.SemaphoreType.DMA((6,))],
        compiler_params=params(),
        cost_estimate=cost(13_000_000),
    )(pos, *flat(got))
    bufs = [[None] * 4 for _ in range(NL)]
    for (l, k), o in zip(ISSUE, outs):
        bufs[l][k] = o
    return bufs


def panel_loads(pos_ref, first, got, x_ref, sem):
    loads = []
    for l in range(NL):
        own = pos_ref[AX.index(ORDERS[l][1])]
        copies = []
        for k in range(4):
            dst = x_ref.at[l, k, 0] if l == 0 else x_ref.at[l, 0, k]
            copies.append(pltpu.make_async_copy(first[l][k].at[own], dst, sem.at[8 * l + k]))
            if k:
                dst = x_ref.at[l, :, k] if l == 0 else x_ref.at[l, k]
                copies.append(pltpu.make_async_copy(got[l][k], dst, sem.at[8 * l + 4 + k]))
        for c in copies:
            c.start()
        loads.append(copies)
    return loads


def panel_kernel(pos_ref, *refs):
    first, got = unflat(refs[:8]), unflat(refs[8:14])
    s_ref = refs[14:16]
    outs = refs[16:24]
    x_ref, s_vmem, acc_ref, u_ref, sem, sem_s, sem_out = refs[24:]
    load_s = []
    for l in range(NL):
        for kz in range(4):
            for k in range(4):
                z, other = lax.rem(pos_ref[0] + kz, 4), lax.rem(pos_ref[1 + l] + k, 4)
                at = 16 * l + 4 * kz + k
                load_s.append(
                    pltpu.make_async_copy(s_ref[l].at[4 * z + other], s_vmem.at[l, kz, k], sem_s.at[at])
                )
                load_s[-1].start()
    loads = panel_loads(pos_ref, first, got, x_ref, sem)
    for c in load_s:
        c.wait()
    stores = []
    for l in range(NL):
        for c in loads[l]:
            c.wait()
        for i in range(2):
            part = lax.dot_general(
                s_vmem[l, 2 * i : 2 * i + 2].reshape(8 * ROWS, KS),
                x_ref[l, 2 * i : 2 * i + 2].reshape(8 * ROWS, LANES),
                (((0,), (0,)), ((), ())),
                preferred_element_type=f32,
            )
            acc_ref[...] = part if i == 0 else acc_ref[...] + part
        u_ref[l] = jnp.transpose(acc_ref[...], (1, 0)).astype(bf16)
        stores += [
            pltpu.make_async_copy(u_ref.at[l, rows], outs[4 * l + k], sem_out.at[4 * l + k])
            for k, rows in strips(pos_ref, l)
        ]
        for c in stores[-4:]:
            c.start()
    for c in stores:
        c.wait()


def strips(pos_ref, l):
    me = pos_ref[AX.index(ORDERS[l][2])]
    return [(k, pl.ds(pl.multiple_of(lax.rem(me + k, 4) * COLS, 16), COLS)) for k in range(4)]


def panel_products(pos, got1, got2, s):
    outs = pl.pallas_call(
        panel_kernel,
        in_specs=[SMEM] + [HBM] * 16,
        out_specs=[HBM] * 8,
        out_shape=[jax.ShapeDtypeStruct((COLS, KS), bf16)] * 8,
        scratch_shapes=[
            pltpu.VMEM((NL, 4, 4, ROWS, LANES), bf16),
            pltpu.VMEM((NL, 4, 4, ROWS, KS), bf16),
            pltpu.VMEM((KS, LANES), f32),
            pltpu.VMEM((NL, LANES, KS), bf16),
            pltpu.SemaphoreType.DMA((16,)),
            pltpu.SemaphoreType.DMA((32,)),
            pltpu.SemaphoreType.DMA((8,)),
        ],
        compiler_params=params(),
        cost_estimate=cost(15_000_000, 4_400_000_000),
    )(pos, *flat(got1), *moved(got2), *s)
    return [list(outs[:4]), list(outs[4:])]


def gram_kernel(*refs):
    got = unflat(refs[:8])
    old_ref, pick_ref = refs[8:10]
    sk_refs, send_ref = refs[10:12], refs[12]
    sums, pieces = [], []
    for l in range(NL):
        parts = [r[...].astype(f32) for r in got[l]]
        sk = (parts[0] + parts[1] + parts[2] + parts[3]).astype(bf16)
        sk_refs[l][...] = sk
        wide = sk.astype(f32)
        diag = jnp.sum(wide * wide, axis=0, keepdims=True)
        high = diag.astype(bf16).astype(f32)
        for d in (high, diag - high):
            pieces += [d[:, 128 * i : 128 * (i + 1)] for i in range(4)]
        chosen = jnp.dot(sk, pick_ref[l], preferred_element_type=f32).astype(bf16)
        right = jnp.concatenate([chosen, old_ref[l]], 1)
        both = lax.dot_general(sk, right, (((0,), (0,)), ((), ())), preferred_element_type=f32)
        sums.append(both.reshape(N, 8, KS))
    send_ref[:, :, 0:KS] = jnp.concatenate(sums, 1).astype(bf16)
    send_ref[:, :, KS : KS + 128] = jnp.broadcast_to(
        jnp.concatenate(pieces, 0).astype(bf16)[None], (N, 16, 128)
    )


def gram_products(got, old, picker):
    outs = pl.pallas_call(
        gram_kernel,
        in_specs=[INNER] * 10,
        out_specs=[INNER] * 3,
        out_shape=[jax.ShapeDtypeStruct((COLS, KS), bf16)] * 2
        + [jax.ShapeDtypeStruct((N, 16, KS + 128), bf16)],
        compiler_params=params(),
        cost_estimate=cost(7_000_000, 1_000_000_000),
    )(*flat(got), old, picker)
    return list(outs[:2]), outs[2]


def back_kernel(pos_ref, *refs):
    first, got = unflat(refs[:8]), unflat(refs[8:14])
    sk_in = unflat(refs[14:22])
    outs = refs[22:30]
    x_ref, sk_ref, t_ref, sem, sem_s, sem_out = refs[30:]
    load_s = []
    for l in range(NL):
        for k, rows in strips(pos_ref, l):
            load_s.append(pltpu.make_async_copy(sk_in[l][k], sk_ref.at[l, rows], sem_s.at[4 * l + k]))
            load_s[-1].start()
    loads = panel_loads(pos_ref, first, got, x_ref, sem)
    for l in range(NL):
        sk_ref[l, WIDE:LANES, :] = jnp.zeros((LANES - WIDE, KS), bf16)
    for c in load_s:
        c.wait()
    stores = []
    for l in range(NL):
        for c in loads[l]:
            c.wait()
        for kz in range(4):
            t_ref[l, kz] = (
                jnp.dot(x_ref[l, kz].reshape(4 * ROWS, LANES), sk_ref[l], preferred_element_type=f32)
                .astype(bf16)
                .reshape(4, ROWS, KS)
            )
            if l == 0:
                stores.append(pltpu.make_async_copy(t_ref.at[0, kz], outs[kz], sem_out.at[kz]))
                stores[-1].start()
                continue
            for k in range(4):
                stores.append(
                    pltpu.make_async_copy(t_ref.at[1, kz, k], outs[4 + k].at[kz], sem_out.at[4 + 4 * kz + k])
                )
                stores[-1].start()
    for c in stores:
        c.wait()


def back_products(pos, got1, got2, sks):
    outs = pl.pallas_call(
        back_kernel,
        in_specs=[SMEM] + [HBM] * 22,
        out_specs=[HBM] * 8,
        out_shape=[jax.ShapeDtypeStruct((4, ROWS, KS), bf16)] * 8,
        scratch_shapes=[
            pltpu.VMEM((NL, 4, 4, ROWS, LANES), bf16),
            pltpu.VMEM((NL, LANES, KS), bf16),
            pltpu.VMEM((NL, 4, 4, ROWS, KS), bf16),
            pltpu.SemaphoreType.DMA((16,)),
            pltpu.SemaphoreType.DMA((8,)),
            pltpu.SemaphoreType.DMA((20,)),
        ],
        compiler_params=params(),
        cost_estimate=cost(16_000_000, 4_400_000_000),
    )(pos, *flat(got1), *moved(got2), *flat(sks))
    return [list(outs[:4]), list(outs[4:])]


def owner_kernel(me_ref, got_ref, ranks_ref, _, mine_ref, scores_ref):
    total = jnp.sum(got_ref[...].astype(f32), axis=0)
    row = me_ref[0] * 8 + lax.broadcasted_iota(jnp.int32, (8, 128), 0)
    lane = lax.broadcasted_iota(jnp.int32, (8, 128), 1)
    my_rows = me_ref[0] * 8 + lax.broadcasted_iota(jnp.int32, (8, RANK), 0)
    owned, scores = [], 0.0
    for l in range(NL):
        diag = total[8 * l : 8 * l + 4, KS:] + total[8 * l + 4 : 8 * l + 8, KS:]
        scores = scores + diag
        trace = jnp.sum(jnp.sum(diag, axis=1, keepdims=True), axis=0, keepdims=True)
        mine = jnp.zeros((8, 128), f32)
        for c in range(4):
            mine = mine + jnp.where(lane + 128 * c == row, diag[c : c + 1, :], 0.0)
        my_diag = jnp.sum(mine, axis=1, keepdims=True)
        scale = 0.5 * KS / trace
        rms = jnp.sqrt(trace / (FF * KS))
        gram = total[8 * l : 8 * l + 8, 0:RANK]
        corrected = jnp.where(my_rows == ranks_ref[l : l + 1, :], 1.5 - scale * my_diag, -scale * gram)
        owned.append(jnp.concatenate([corrected / rms, total[8 * l : 8 * l + 8, RANK:KS]], 1))
    mine_ref[...] = jnp.broadcast_to(jnp.concatenate(owned, 0).astype(bf16)[None], (N, 16, KS))
    scores_ref[...] = scores / FF


def owner_rows(me, got, ranks, earlier):
    return pl.pallas_call(
        owner_kernel,
        in_specs=[SMEM, INNER, INNER, HBM],
        out_specs=[INNER, INNER],
        out_shape=[jax.ShapeDtypeStruct((N, 16, KS), bf16), jax.ShapeDtypeStruct((4, 128), f32)],
        compiler_params=params(),
        cost_estimate=cost(2_500_000),
    )(me, got, ranks, earlier)


def moments_kernel(rows_ref, sk0_ref, sk1_ref, one_ref, two_ref, basis_ref, first_ref, second_ref, factor_ref):
    rows = rows_ref[...].astype(f32)
    for l in range(NL):
        both = rows[:, 8 * l : 8 * l + 8, :].reshape(KS, KS).astype(bf16)
        factor, inner = both[:, :RANK], both[:, RANK:]
        factor_ref[l] = factor
        sk = (sk0_ref, sk1_ref)[l][...]
        basis_ref[l] = jnp.dot(sk, factor, preferred_element_type=f32).astype(bf16)
        correlation = lax.dot_general(
            inner, factor, (((0,), (0,)), ((), ())), preferred_element_type=f32
        ) / math.sqrt(FF * RANK)
        first_ref[l] = jnp.dot(one_ref[l], correlation, precision=highest, preferred_element_type=f32)
        second_ref[l] = jnp.dot(
            two_ref[l], correlation * correlation, precision=highest, preferred_element_type=f32
        )


def moments(rows, sk, one, two):
    return pl.pallas_call(
        moments_kernel,
        in_specs=[INNER] * 5,
        out_specs=[INNER] * 4,
        out_shape=[
            jax.ShapeDtypeStruct((NL, COLS, RANK), bf16),
            jax.ShapeDtypeStruct((NL, ROWS, RANK), f32),
            jax.ShapeDtypeStruct((NL, ROWS, RANK), f32),
            jax.ShapeDtypeStruct((NL, KS, RANK), bf16),
        ],
        compiler_params=params(),
        cost_estimate=cost(4_000_000, 500_000_000),
    )(rows, *sk, one, two)


def project_kernel(*refs):
    got = unflat(refs[:8])
    factor_ref, out_ref = refs[8:]
    for l in range(NL):
        t_rows = sum(got[l][k][...].astype(f32) for k in range(4))
        out_ref[l] = (
            jnp.dot(t_rows, factor_ref[l].astype(f32), precision=highest, preferred_element_type=f32)
            / math.sqrt(FF)
        ).astype(bf16)


def project(got, factor):
    return pl.pallas_call(
        project_kernel,
        in_specs=[INNER] * 9,
        out_specs=INNER,
        out_shape=jax.ShapeDtypeStruct((NL, ROWS, RANK), bf16),
        compiler_params=params(),
        cost_estimate=cost(2_000_000, 100_000_000),
    )(*flat(got), factor)


def reduce_kernel(*refs):
    got = unflat(refs[:8])
    outs = refs[8:]
    for l in range(NL):
        for k in range(4):
            outs[4 * l + k][...] = sum(got[l][j][k].astype(f32) for j in range(4)).astype(bf16)


def reduce_stage(got):
    outs = pl.pallas_call(
        reduce_kernel,
        in_specs=[INNER] * 8,
        out_specs=[INNER] * 8,
        out_shape=[jax.ShapeDtypeStruct((ROWS, KS), bf16)] * 8,
        compiler_params=params(),
        cost_estimate=cost(3_300_000),
    )(*flat(got))
    return [list(outs[:4]), list(outs[4:])]


def shift_back(bufs, stage):
    got = [[b[0], None, None, None] for b in bufs]
    for l, k in ISSUE:
        got[l][k] = shifted(bufs[l][4 - k], ORDERS[l][stage], k)
    return got


def shards(gradients, sketch, rank_lists, old_basis, first_moment, second_moment):
    s_rows = [lax.all_gather(sketch, axes, axis=0) for axes in (("z", "x"), ("z", "y"))]
    pos = jnp.stack([lax.axis_index(a) for a in AX]).astype(jnp.int32)
    got1 = permute_stage(pack(pos, gradients), 0)
    got2 = permute_stage(second(pos, got1), 1)
    picker = (lax.broadcasted_iota(jnp.int32, (NL, KS, RANK), 1) == rank_lists[:, None, :]).astype(bf16)
    parts = shift_back(panel_products(pos, got1, got2, s_rows), 2)
    sketched, send = gram_products(parts, old_basis, picker)
    got = lax.all_to_all(send, AX, 0, 0, tiled=True)
    sks = permute_stage([[sk] * 4 for sk in sketched], 2)
    me = (16 * pos[0] + 4 * pos[1] + pos[2])[None]
    mine, scores = owner_rows(me, got, rank_lists, sks[1][1])
    everyone = lax.all_to_all(mine, AX, 0, 0, tiled=True)
    basis, first, second_out, factor = moments(everyone, sketched, first_moment, second_moment)
    back = shift_back(back_products(pos, got1, got2, sks), 0)
    back = shift_back(reduce_stage(back), 1)
    projected = project(back, factor)
    scores = scores + lax.ppermute(scores, "layer", [(0, 1), (1, 0)])
    return basis, projected, first, second_out, scores.reshape(KS)


def solution(mesh):
    cube = Mesh(mesh.devices.reshape(4, 4, 4, 2), AX + ("layer",))
    rows = P("layer", AX, None)
    return jax.shard_map(
        shards,
        mesh=cube,
        in_specs=(rows, P(AX, None), P("layer", None), rows, rows, rows),
        out_specs=(rows, rows, rows, rows, P()),
        check_vma=False,
    )
```

```python
import math

import jax
import jax.numpy as jnp
from jax import lax
from jax.experimental import pallas as pl
from jax.experimental.pallas import tpu as pltpu
from jax.sharding import Mesh, PartitionSpec as P

FF = 25600
KS = 512
RANK = 256
ROWS = 80
COLS = 400
NL = 2
N = 64
WIDE = 4 * COLS
LANES = 1664

bf16 = jnp.bfloat16
f32 = jnp.float32
highest = lax.Precision.HIGHEST
AX = ("z", "x", "y")
VMEM = 56 * 1024 * 1024

ORDERS = (("z", "x", "y"), ("y", "z", "x"))
ISSUE = ((1, 1), (1, 3), (0, 1), (0, 3), (0, 2), (1, 2))
FIRST = ((0, 1), (0, 3), (1, 1), (1, 3), (1, 2), (0, 2))
HBM = pl.BlockSpec(memory_space=pl.ANY)
SMEM = pl.BlockSpec(memory_space=pltpu.SMEM)
INNER = pl.BlockSpec(memory_space=pltpu.VMEM)


def shifted(x, axis, k):
    return lax.ppermute(x, axis, [(s, (s - k) % 4) for s in range(4)])


def params():
    return pltpu.CompilerParams(vmem_limit_bytes=VMEM)


def cost(nbytes, flops=0):
    return pl.CostEstimate(flops=flops, bytes_accessed=nbytes, transcendentals=0)


def pack_kernel(pos_ref, g_ref, *refs):
    outs, scr, sem = refs[:8], refs[8:10], refs[10]
    z = pl.program_id(0)
    kz = lax.rem(pos_ref[0] - z + 4, 4)

    def put(block, strips):
        wide = jnp.concatenate(strips + [jnp.zeros((ROWS, LANES - WIDE), bf16)], axis=1)
        block[...] = wide

    for i in range(4):
        put(scr[0].at[kz, i], [g_ref[0, :, WIDE * i : WIDE * (i + 1)]])
        ky = lax.rem(pos_ref[2] - i + 4, 4)
        put(
            scr[1].at[ky, z],
            [g_ref[1, :, WIDE * x + COLS * i : WIDE * x + COLS * (i + 1)] for x in range(4)],
        )
    for k in range(4):

        @pl.when(kz == k)
        def _():
            pltpu.make_async_copy(scr[0].at[k], outs[k], sem.at[k]).start()

        pltpu.make_async_copy(scr[1].at[k, z], outs[4 + k].at[z], sem.at[4 + k]).start()

    @pl.when(z == 3)
    def _():
        for l in range(NL):
            for k in range(4):
                pltpu.make_async_copy(scr[l].at[k], outs[4 * l + k], sem.at[4 * l + k]).wait()


def pack(pos, g):
    outs = pl.pallas_call(
        pack_kernel,
        grid=(4,),
        in_specs=[SMEM, pl.BlockSpec((NL, ROWS, 4 * WIDE), lambda i: (0, 0, i))],
        out_specs=[HBM] * 8,
        out_shape=[jax.ShapeDtypeStruct((4, ROWS, LANES), bf16)] * 8,
        scratch_shapes=[pltpu.VMEM((4, 4, ROWS, LANES), bf16)] * 2 + [pltpu.SemaphoreType.DMA((8,))],
        compiler_params=params(),
        cost_estimate=cost(17_000_000),
    )(pos, g)
    return [list(outs[:4]), list(outs[4:])]


def permute_stage(bufs, stage, order=ISSUE):
    got = [[b[0], None, None, None] for b in bufs]
    for l, k in order:
        got[l][k] = shifted(bufs[l][k], ORDERS[l][stage], k)
    return got


def moved(got, order=ISSUE):
    return [got[l][k] for l, k in order]


def flat(got, order=ISSUE):
    return moved(got, order) + [got[l][0] for l in range(NL)]


def unflat(refs, order=ISSUE):
    got = [[None] * 4 for _ in range(NL)]
    for (l, k), r in zip(order, refs):
        got[l][k] = r
    for l, r in enumerate(refs[6:]):
        got[l][0] = r
    return got


def second_kernel(pos_ref, *refs):
    first = unflat(refs[:8], FIRST)
    outs, scr, sem, sem_out = refs[8:14], refs[14:20], refs[20], refs[21]
    loads = [[] for _ in outs]
    for at, (l, k) in enumerate(ISSUE):
        place = lax.rem(pos_ref[AX.index(ORDERS[l][1])] + 4 - k, 4)
        for k1 in range(4):
            loads[at].append(
                pltpu.make_async_copy(first[l][k1].at[place], scr[at].at[k1], sem.at[4 * at + k1])
            )
    for group in loads:
        for c in group:
            c.start()
    stores = []
    for at, group in enumerate(loads):
        for c in group:
            c.wait()
        stores.append(pltpu.make_async_copy(scr[at], outs[at], sem_out.at[at]))
        stores[-1].start()
    for c in stores:
        c.wait()


def second(pos, got):
    outs = pl.pallas_call(
        second_kernel,
        in_specs=[SMEM] + [HBM] * 8,
        out_specs=[HBM] * 6,
        out_shape=[jax.ShapeDtypeStruct((4, ROWS, LANES), bf16)] * 6,
        scratch_shapes=[pltpu.VMEM((4, ROWS, LANES), bf16)] * 6
        + [pltpu.SemaphoreType.DMA((24,)), pltpu.SemaphoreType.DMA((6,))],
        compiler_params=params(),
        cost_estimate=cost(13_000_000),
    )(pos, *flat(got, FIRST))
    bufs = [[None] * 4 for _ in range(NL)]
    for (l, k), o in zip(ISSUE, outs):
        bufs[l][k] = o
    return bufs


def panel_loads(pos_ref, first, got, x_ref, sem):
    loads = []
    for l in range(NL):
        own = pos_ref[AX.index(ORDERS[l][1])]
        copies = []
        for k in range(4):
            dst = x_ref.at[l, k, 0] if l == 0 else x_ref.at[l, 0, k]
            copies.append(pltpu.make_async_copy(first[l][k].at[own], dst, sem.at[8 * l + k]))
            if k:
                dst = x_ref.at[l, :, k] if l == 0 else x_ref.at[l, k]
                copies.append(pltpu.make_async_copy(got[l][k], dst, sem.at[8 * l + 4 + k]))
        for c in copies:
            c.start()
        loads.append(copies)
    return loads


def panel_kernel(pos_ref, *refs):
    first, got = unflat(refs[:8], FIRST), unflat(refs[8:14])
    s_ref = refs[14:16]
    outs = refs[16:24]
    x_ref, s_vmem, acc_ref, u_ref, sem, sem_s, sem_out = refs[24:]
    load_s = []
    for l in range(NL):
        for kz in range(4):
            for k in range(4):
                z, other = lax.rem(pos_ref[0] + kz, 4), lax.rem(pos_ref[1 + l] + k, 4)
                at = 16 * l + 4 * kz + k
                load_s.append(
                    pltpu.make_async_copy(s_ref[l].at[4 * z + other], s_vmem.at[l, kz, k], sem_s.at[at])
                )
                load_s[-1].start()
    loads = panel_loads(pos_ref, first, got, x_ref, sem)
    for c in load_s:
        c.wait()
    stores = []
    for l in range(NL):
        for c in loads[l]:
            c.wait()
        for i in range(2):
            part = lax.dot_general(
                s_vmem[l, 2 * i : 2 * i + 2].reshape(8 * ROWS, KS),
                x_ref[l, 2 * i : 2 * i + 2].reshape(8 * ROWS, LANES),
                (((0,), (0,)), ((), ())),
                preferred_element_type=f32,
            )
            acc_ref[...] = part if i == 0 else acc_ref[...] + part
        u_ref[l] = jnp.transpose(acc_ref[...], (1, 0)).astype(bf16)
        stores += [
            pltpu.make_async_copy(u_ref.at[l, rows], outs[4 * l + k], sem_out.at[4 * l + k])
            for k, rows in strips(pos_ref, l)
        ]
        for c in stores[-4:]:
            c.start()
    for c in stores:
        c.wait()


def strips(pos_ref, l):
    me = pos_ref[AX.index(ORDERS[l][2])]
    return [(k, pl.ds(pl.multiple_of(lax.rem(me + k, 4) * COLS, 16), COLS)) for k in range(4)]


def panel_products(pos, got1, got2, s):
    outs = pl.pallas_call(
        panel_kernel,
        in_specs=[SMEM] + [HBM] * 16,
        out_specs=[HBM] * 8,
        out_shape=[jax.ShapeDtypeStruct((COLS, KS), bf16)] * 8,
        scratch_shapes=[
            pltpu.VMEM((NL, 4, 4, ROWS, LANES), bf16),
            pltpu.VMEM((NL, 4, 4, ROWS, KS), bf16),
            pltpu.VMEM((KS, LANES), f32),
            pltpu.VMEM((NL, LANES, KS), bf16),
            pltpu.SemaphoreType.DMA((16,)),
            pltpu.SemaphoreType.DMA((32,)),
            pltpu.SemaphoreType.DMA((8,)),
        ],
        compiler_params=params(),
        cost_estimate=cost(15_000_000, 4_400_000_000),
    )(pos, *flat(got1, FIRST), *moved(got2), *s)
    return [list(outs[:4]), list(outs[4:])]


def gram_kernel(*refs):
    got = unflat(refs[:8])
    old_ref, pick_ref = refs[8:10]
    sk_refs, send_ref = refs[10:12], refs[12]
    sums, pieces = [], []
    for l in range(NL):
        parts = [r[...].astype(f32) for r in got[l]]
        sk = (parts[0] + parts[1] + parts[2] + parts[3]).astype(bf16)
        sk_refs[l][...] = sk
        wide = sk.astype(f32)
        diag = jnp.sum(wide * wide, axis=0, keepdims=True)
        high = diag.astype(bf16).astype(f32)
        for d in (high, diag - high):
            pieces += [d[:, 128 * i : 128 * (i + 1)] for i in range(4)]
        chosen = jnp.dot(sk, pick_ref[l], preferred_element_type=f32).astype(bf16)
        right = jnp.concatenate([chosen, old_ref[l]], 1)
        both = lax.dot_general(sk, right, (((0,), (0,)), ((), ())), preferred_element_type=f32)
        sums.append(both.reshape(N, 8, KS))
    send_ref[:, :, 0:KS] = jnp.concatenate(sums, 1).astype(bf16)
    send_ref[:, :, KS : KS + 128] = jnp.broadcast_to(
        jnp.concatenate(pieces, 0).astype(bf16)[None], (N, 16, 128)
    )


def gram_products(got, old, picker):
    outs = pl.pallas_call(
        gram_kernel,
        in_specs=[INNER] * 10,
        out_specs=[INNER] * 3,
        out_shape=[jax.ShapeDtypeStruct((COLS, KS), bf16)] * 2
        + [jax.ShapeDtypeStruct((N, 16, KS + 128), bf16)],
        compiler_params=params(),
        cost_estimate=cost(7_000_000, 1_000_000_000),
    )(*flat(got), old, picker)
    return list(outs[:2]), outs[2]


def back_kernel(pos_ref, *refs):
    first, got = unflat(refs[:8], FIRST), unflat(refs[8:14])
    sk_in = unflat(refs[14:22])
    outs = refs[22:30]
    x_ref, sk_ref, t_ref, sem, sem_s, sem_out = refs[30:]
    load_s = []
    for l in range(NL):
        for k, rows in strips(pos_ref, l):
            load_s.append(pltpu.make_async_copy(sk_in[l][k], sk_ref.at[l, rows], sem_s.at[4 * l + k]))
            load_s[-1].start()
    loads = panel_loads(pos_ref, first, got, x_ref, sem)
    for l in range(NL):
        sk_ref[l, WIDE:LANES, :] = jnp.zeros((LANES - WIDE, KS), bf16)
    for c in load_s:
        c.wait()
    stores = []
    for l in range(NL):
        for c in loads[l]:
            c.wait()
        for kz in range(4):
            t_ref[l, kz] = (
                jnp.dot(x_ref[l, kz].reshape(4 * ROWS, LANES), sk_ref[l], preferred_element_type=f32)
                .astype(bf16)
                .reshape(4, ROWS, KS)
            )
            if l == 0:
                stores.append(pltpu.make_async_copy(t_ref.at[0, kz], outs[kz], sem_out.at[kz]))
                stores[-1].start()
                continue
            for k in range(4):
                stores.append(
                    pltpu.make_async_copy(t_ref.at[1, kz, k], outs[4 + k].at[kz], sem_out.at[4 + 4 * kz + k])
                )
                stores[-1].start()
    for c in stores:
        c.wait()


def back_products(pos, got1, got2, sks):
    outs = pl.pallas_call(
        back_kernel,
        in_specs=[SMEM] + [HBM] * 22,
        out_specs=[HBM] * 8,
        out_shape=[jax.ShapeDtypeStruct((4, ROWS, KS), bf16)] * 8,
        scratch_shapes=[
            pltpu.VMEM((NL, 4, 4, ROWS, LANES), bf16),
            pltpu.VMEM((NL, LANES, KS), bf16),
            pltpu.VMEM((NL, 4, 4, ROWS, KS), bf16),
            pltpu.SemaphoreType.DMA((16,)),
            pltpu.SemaphoreType.DMA((8,)),
            pltpu.SemaphoreType.DMA((20,)),
        ],
        compiler_params=params(),
        cost_estimate=cost(16_000_000, 4_400_000_000),
    )(pos, *flat(got1, FIRST), *moved(got2), *flat(sks))
    return [list(outs[:4]), list(outs[4:])]


def owner_kernel(me_ref, got_ref, ranks_ref, _, mine_ref, scores_ref):
    total = jnp.sum(got_ref[...].astype(f32), axis=0)
    row = me_ref[0] * 8 + lax.broadcasted_iota(jnp.int32, (8, 128), 0)
    lane = lax.broadcasted_iota(jnp.int32, (8, 128), 1)
    my_rows = me_ref[0] * 8 + lax.broadcasted_iota(jnp.int32, (8, RANK), 0)
    owned, scores = [], 0.0
    for l in range(NL):
        diag = total[8 * l : 8 * l + 4, KS:] + total[8 * l + 4 : 8 * l + 8, KS:]
        scores = scores + diag
        trace = jnp.sum(jnp.sum(diag, axis=1, keepdims=True), axis=0, keepdims=True)
        mine = jnp.zeros((8, 128), f32)
        for c in range(4):
            mine = mine + jnp.where(lane + 128 * c == row, diag[c : c + 1, :], 0.0)
        my_diag = jnp.sum(mine, axis=1, keepdims=True)
        scale = 0.5 * KS / trace
        rms = jnp.sqrt(trace / (FF * KS))
        gram = total[8 * l : 8 * l + 8, 0:RANK]
        corrected = jnp.where(my_rows == ranks_ref[l : l + 1, :], 1.5 - scale * my_diag, -scale * gram)
        owned.append(jnp.concatenate([corrected / rms, total[8 * l : 8 * l + 8, RANK:KS]], 1))
    mine_ref[...] = jnp.broadcast_to(jnp.concatenate(owned, 0).astype(bf16)[None], (N, 16, KS))
    scores_ref[...] = scores / FF


def owner_rows(me, got, ranks, earlier):
    return pl.pallas_call(
        owner_kernel,
        in_specs=[SMEM, INNER, INNER, HBM],
        out_specs=[INNER, INNER],
        out_shape=[jax.ShapeDtypeStruct((N, 16, KS), bf16), jax.ShapeDtypeStruct((4, 128), f32)],
        compiler_params=params(),
        cost_estimate=cost(2_500_000),
    )(me, got, ranks, earlier)


def moments_kernel(rows_ref, sk0_ref, sk1_ref, one_ref, two_ref, basis_ref, first_ref, second_ref, factor_ref):
    rows = rows_ref[...].astype(f32)
    for l in range(NL):
        both = rows[:, 8 * l : 8 * l + 8, :].reshape(KS, KS).astype(bf16)
        factor, inner = both[:, :RANK], both[:, RANK:]
        factor_ref[l] = factor
        sk = (sk0_ref, sk1_ref)[l][...]
        basis_ref[l] = jnp.dot(sk, factor, preferred_element_type=f32).astype(bf16)
        correlation = lax.dot_general(
            inner, factor, (((0,), (0,)), ((), ())), preferred_element_type=f32
        ) / math.sqrt(FF * RANK)
        first_ref[l] = jnp.dot(one_ref[l], correlation, precision=highest, preferred_element_type=f32)
        second_ref[l] = jnp.dot(
            two_ref[l], correlation * correlation, precision=highest, preferred_element_type=f32
        )


def moments(rows, sk, one, two):
    return pl.pallas_call(
        moments_kernel,
        in_specs=[INNER] * 5,
        out_specs=[INNER] * 4,
        out_shape=[
            jax.ShapeDtypeStruct((NL, COLS, RANK), bf16),
            jax.ShapeDtypeStruct((NL, ROWS, RANK), f32),
            jax.ShapeDtypeStruct((NL, ROWS, RANK), f32),
            jax.ShapeDtypeStruct((NL, KS, RANK), bf16),
        ],
        compiler_params=params(),
        cost_estimate=cost(4_000_000, 500_000_000),
    )(rows, *sk, one, two)


def project_kernel(*refs):
    got = unflat(refs[:8])
    factor_ref, out_ref = refs[8:]
    for l in range(NL):
        t_rows = sum(got[l][k][...].astype(f32) for k in range(4))
        out_ref[l] = (
            jnp.dot(t_rows, factor_ref[l].astype(f32), precision=highest, preferred_element_type=f32)
            / math.sqrt(FF)
        ).astype(bf16)


def project(got, factor):
    return pl.pallas_call(
        project_kernel,
        in_specs=[INNER] * 9,
        out_specs=INNER,
        out_shape=jax.ShapeDtypeStruct((NL, ROWS, RANK), bf16),
        compiler_params=params(),
        cost_estimate=cost(2_000_000, 100_000_000),
    )(*flat(got), factor)


def reduce_kernel(*refs):
    got = unflat(refs[:8])
    outs = refs[8:]
    for l in range(NL):
        for k in range(4):
            outs[4 * l + k][...] = sum(got[l][j][k].astype(f32) for j in range(4)).astype(bf16)


def reduce_stage(got):
    outs = pl.pallas_call(
        reduce_kernel,
        in_specs=[INNER] * 8,
        out_specs=[INNER] * 8,
        out_shape=[jax.ShapeDtypeStruct((ROWS, KS), bf16)] * 8,
        compiler_params=params(),
        cost_estimate=cost(3_300_000),
    )(*flat(got))
    return [list(outs[:4]), list(outs[4:])]


def shift_back(bufs, stage):
    got = [[b[0], None, None, None] for b in bufs]
    for l, k in ISSUE:
        got[l][k] = shifted(bufs[l][4 - k], ORDERS[l][stage], k)
    return got


def shards(gradients, sketch, rank_lists, old_basis, first_moment, second_moment):
    s_rows = [lax.all_gather(sketch, axes, axis=0) for axes in (("z", "x"), ("z", "y"))]
    pos = jnp.stack([lax.axis_index(a) for a in AX]).astype(jnp.int32)
    got1 = permute_stage(pack(pos, gradients), 0, FIRST)
    got2 = permute_stage(second(pos, got1), 1)
    picker = (lax.broadcasted_iota(jnp.int32, (NL, KS, RANK), 1) == rank_lists[:, None, :]).astype(bf16)
    parts = shift_back(panel_products(pos, got1, got2, s_rows), 2)
    sketched, send = gram_products(parts, old_basis, picker)
    got = lax.all_to_all(send, AX, 0, 0, tiled=True)
    sks = permute_stage([[sk] * 4 for sk in sketched], 2)
    me = (16 * pos[0] + 4 * pos[1] + pos[2])[None]
    mine, scores = owner_rows(me, got, rank_lists, sks[1][1])
    everyone = lax.all_to_all(mine, AX, 0, 0, tiled=True)
    basis, first, second_out, factor = moments(everyone, sketched, first_moment, second_moment)
    back = shift_back(back_products(pos, got1, got2, sks), 0)
    back = shift_back(reduce_stage(back), 1)
    projected = project(back, factor)
    scores = scores + lax.ppermute(scores, "layer", [(0, 1), (1, 0)])
    return basis, projected, first, second_out, scores.reshape(KS)


def solution(mesh):
    cube = Mesh(mesh.devices.reshape(4, 4, 4, 2), AX + ("layer",))
    rows = P("layer", AX, None)
    return jax.shard_map(
        shards,
        mesh=cube,
        in_specs=(rows, P(AX, None), P("layer", None), rows, rows, rows),
        out_specs=(rows, rows, rows, rows, P()),
        check_vma=False,
    )
```

```python
import math

import jax
import jax.numpy as jnp
from jax import lax
from jax.experimental import pallas as pl
from jax.experimental.pallas import tpu as pltpu
from jax.sharding import Mesh, PartitionSpec as P

FF = 25600
KS = 512
RANK = 256
ROWS = 80
COLS = 400
NL = 2
N = 64
WIDE = 4 * COLS
LANES = 1664

bf16 = jnp.bfloat16
f32 = jnp.float32
highest = lax.Precision.HIGHEST
AX = ("z", "x", "y")
VMEM = 56 * 1024 * 1024

ORDERS = (("z", "x", "y"), ("y", "z", "x"))
ISSUE = ((1, 1), (1, 3), (0, 1), (0, 3), (0, 2), (1, 2))
FIRST = ((0, 1), (0, 3), (1, 1), (1, 3), (1, 2), (0, 2))
HBM = pl.BlockSpec(memory_space=pl.ANY)
SMEM = pl.BlockSpec(memory_space=pltpu.SMEM)
INNER = pl.BlockSpec(memory_space=pltpu.VMEM)


def shifted(x, axis, k):
    return lax.ppermute(x, axis, [(s, (s - k) % 4) for s in range(4)])


def params():
    return pltpu.CompilerParams(vmem_limit_bytes=VMEM)


def cost(nbytes, flops=0):
    return pl.CostEstimate(flops=flops, bytes_accessed=nbytes, transcendentals=0)


def pack_kernel(pos_ref, g_ref, *refs):
    outs, scr, sem = refs[:8], refs[8:10], refs[10]
    z = pl.program_id(0)
    kz = lax.rem(pos_ref[0] - z + 4, 4)

    def put(block, strips):
        wide = jnp.concatenate(strips + [jnp.zeros((ROWS, LANES - WIDE), bf16)], axis=1)
        block[...] = wide

    @pl.when(pl.program_id(1) == 0)
    def _():
        for i in range(4):
            put(scr[0].at[kz, i], [g_ref[0, :, WIDE * i : WIDE * (i + 1)]])
        for k in range(4):

            @pl.when(kz == k)
            def _():
                pltpu.make_async_copy(scr[0].at[k], outs[k], sem.at[k]).start()

    @pl.when(pl.program_id(1) == 1)
    def _():
        for i in range(4):
            ky = lax.rem(pos_ref[2] - i + 4, 4)
            put(
                scr[1].at[ky, z],
                [g_ref[0, :, WIDE * x + COLS * i : WIDE * x + COLS * (i + 1)] for x in range(4)],
            )
        for k in range(4):
            pltpu.make_async_copy(scr[1].at[k, z], outs[4 + k].at[z], sem.at[4 + k]).start()

    @pl.when((z == 3) & (pl.program_id(1) == 1))
    def _():
        for l in range(NL):
            for k in range(4):
                pltpu.make_async_copy(scr[l].at[k], outs[4 * l + k], sem.at[4 * l + k]).wait()


def pack(pos, g):
    outs = pl.pallas_call(
        pack_kernel,
        grid=(4, NL),
        in_specs=[SMEM, pl.BlockSpec((1, ROWS, 4 * WIDE), lambda i, l: (l, 0, i))],
        out_specs=[HBM] * 8,
        out_shape=[jax.ShapeDtypeStruct((4, ROWS, LANES), bf16)] * 8,
        scratch_shapes=[pltpu.VMEM((4, 4, ROWS, LANES), bf16)] * 2 + [pltpu.SemaphoreType.DMA((8,))],
        compiler_params=params(),
        cost_estimate=cost(17_000_000),
    )(pos, g)
    return [list(outs[:4]), list(outs[4:])]


def permute_stage(bufs, stage, order=ISSUE):
    got = [[b[0], None, None, None] for b in bufs]
    for l, k in order:
        got[l][k] = shifted(bufs[l][k], ORDERS[l][stage], k)
    return got


def moved(got, order=ISSUE):
    return [got[l][k] for l, k in order]


def flat(got, order=ISSUE):
    return moved(got, order) + [got[l][0] for l in range(NL)]


def unflat(refs, order=ISSUE):
    got = [[None] * 4 for _ in range(NL)]
    for (l, k), r in zip(order, refs):
        got[l][k] = r
    for l, r in enumerate(refs[6:]):
        got[l][0] = r
    return got


def second_kernel(pos_ref, *refs):
    first = unflat(refs[:8], FIRST)
    outs, scr, sem, sem_out = refs[8:14], refs[14:20], refs[20], refs[21]
    loads = [[] for _ in outs]
    for at, (l, k) in enumerate(ISSUE):
        place = lax.rem(pos_ref[AX.index(ORDERS[l][1])] + 4 - k, 4)
        for k1 in range(4):
            loads[at].append(
                pltpu.make_async_copy(first[l][k1].at[place], scr[at].at[k1], sem.at[4 * at + k1])
            )
    for group in loads:
        for c in group:
            c.start()
    stores = []
    for at, group in enumerate(loads):
        for c in group:
            c.wait()
        stores.append(pltpu.make_async_copy(scr[at], outs[at], sem_out.at[at]))
        stores[-1].start()
    for c in stores:
        c.wait()


def second(pos, got):
    outs = pl.pallas_call(
        second_kernel,
        in_specs=[SMEM] + [HBM] * 8,
        out_specs=[HBM] * 6,
        out_shape=[jax.ShapeDtypeStruct((4, ROWS, LANES), bf16)] * 6,
        scratch_shapes=[pltpu.VMEM((4, ROWS, LANES), bf16)] * 6
        + [pltpu.SemaphoreType.DMA((24,)), pltpu.SemaphoreType.DMA((6,))],
        compiler_params=params(),
        cost_estimate=cost(13_000_000),
    )(pos, *flat(got, FIRST))
    bufs = [[None] * 4 for _ in range(NL)]
    for (l, k), o in zip(ISSUE, outs):
        bufs[l][k] = o
    return bufs


def panel_loads(pos_ref, first, got, x_ref, sem):
    loads = []
    for l in range(NL):
        own = pos_ref[AX.index(ORDERS[l][1])]
        copies = []
        for k in range(4):
            dst = x_ref.at[l, k, 0] if l == 0 else x_ref.at[l, 0, k]
            copies.append(pltpu.make_async_copy(first[l][k].at[own], dst, sem.at[8 * l + k]))
            if k:
                dst = x_ref.at[l, :, k] if l == 0 else x_ref.at[l, k]
                copies.append(pltpu.make_async_copy(got[l][k], dst, sem.at[8 * l + 4 + k]))
        for c in copies:
            c.start()
        loads.append(copies)
    return loads


def panel_kernel(pos_ref, *refs):
    first, got = unflat(refs[:8], FIRST), unflat(refs[8:14])
    s_ref = refs[14:16]
    outs = refs[16:24]
    x_ref, s_vmem, acc_ref, u_ref, sem, sem_s, sem_out = refs[24:]
    loads = panel_loads(pos_ref, first, got, x_ref, sem)
    load_s = []
    for l in range(NL):
        for kz in range(4):
            for k in range(4):
                z, other = lax.rem(pos_ref[0] + kz, 4), lax.rem(pos_ref[1 + l] + k, 4)
                at = 16 * l + 4 * kz + k
                load_s.append(
                    pltpu.make_async_copy(s_ref[l].at[4 * z + other], s_vmem.at[l, kz, k], sem_s.at[at])
                )
                load_s[-1].start()
    stores = []
    for l in range(NL):
        for c in loads[l] + load_s[16 * l : 16 * l + 16]:
            c.wait()
        for i in range(2):
            part = lax.dot_general(
                s_vmem[l, 2 * i : 2 * i + 2].reshape(8 * ROWS, KS),
                x_ref[l, 2 * i : 2 * i + 2].reshape(8 * ROWS, LANES),
                (((0,), (0,)), ((), ())),
                preferred_element_type=f32,
            )
            acc_ref[...] = part if i == 0 else acc_ref[...] + part
        u_ref[l] = jnp.transpose(acc_ref[...], (1, 0)).astype(bf16)
        stores += [
            pltpu.make_async_copy(u_ref.at[l, rows], outs[4 * l + k], sem_out.at[4 * l + k])
            for k, rows in strips(pos_ref, l)
        ]
        for c in stores[-4:]:
            c.start()
    for c in stores:
        c.wait()


def strips(pos_ref, l):
    me = pos_ref[AX.index(ORDERS[l][2])]
    return [(k, pl.ds(pl.multiple_of(lax.rem(me + k, 4) * COLS, 16), COLS)) for k in range(4)]


def panel_products(pos, got1, got2, s):
    outs = pl.pallas_call(
        panel_kernel,
        in_specs=[SMEM] + [HBM] * 16,
        out_specs=[HBM] * 8,
        out_shape=[jax.ShapeDtypeStruct((COLS, KS), bf16)] * 8,
        scratch_shapes=[
            pltpu.VMEM((NL, 4, 4, ROWS, LANES), bf16),
            pltpu.VMEM((NL, 4, 4, ROWS, KS), bf16),
            pltpu.VMEM((KS, LANES), f32),
            pltpu.VMEM((NL, LANES, KS), bf16),
            pltpu.SemaphoreType.DMA((16,)),
            pltpu.SemaphoreType.DMA((32,)),
            pltpu.SemaphoreType.DMA((8,)),
        ],
        compiler_params=params(),
        cost_estimate=cost(15_000_000, 4_400_000_000),
    )(pos, *flat(got1, FIRST), *moved(got2), *s)
    return [list(outs[:4]), list(outs[4:])]


def gram_kernel(*refs):
    got = unflat(refs[:8])
    old_ref, pick_ref = refs[8:10]
    sk_refs, send_ref = refs[10:12], refs[12]
    sums, pieces = [], []
    for l in range(NL):
        parts = [r[...].astype(f32) for r in got[l]]
        sk = (parts[0] + parts[1] + parts[2] + parts[3]).astype(bf16)
        sk_refs[l][...] = sk
        wide = sk.astype(f32)
        diag = jnp.sum(wide * wide, axis=0, keepdims=True)
        high = diag.astype(bf16).astype(f32)
        for d in (high, diag - high):
            pieces += [d[:, 128 * i : 128 * (i + 1)] for i in range(4)]
        chosen = jnp.dot(sk, pick_ref[l], preferred_element_type=f32).astype(bf16)
        right = jnp.concatenate([chosen, old_ref[l]], 1)
        both = lax.dot_general(sk, right, (((0,), (0,)), ((), ())), preferred_element_type=f32)
        sums.append(both.reshape(N, 8, KS))
    send_ref[:, :, 0:KS] = jnp.concatenate(sums, 1).astype(bf16)
    send_ref[:, :, KS : KS + 128] = jnp.broadcast_to(
        jnp.concatenate(pieces, 0).astype(bf16)[None], (N, 16, 128)
    )


def gram_products(got, old, picker):
    outs = pl.pallas_call(
        gram_kernel,
        in_specs=[INNER] * 10,
        out_specs=[INNER] * 3,
        out_shape=[jax.ShapeDtypeStruct((COLS, KS), bf16)] * 2
        + [jax.ShapeDtypeStruct((N, 16, KS + 128), bf16)],
        compiler_params=params(),
        cost_estimate=cost(7_000_000, 1_000_000_000),
    )(*flat(got), old, picker)
    return list(outs[:2]), outs[2]


def back_kernel(pos_ref, *refs):
    first, got = unflat(refs[:8], FIRST), unflat(refs[8:14])
    sk_in = unflat(refs[14:22])
    outs = refs[22:30]
    x_ref, sk_ref, t_ref, sem, sem_s, sem_out = refs[30:]
    load_s = []
    for l in range(NL):
        for k, rows in strips(pos_ref, l):
            load_s.append(pltpu.make_async_copy(sk_in[l][k], sk_ref.at[l, rows], sem_s.at[4 * l + k]))
            load_s[-1].start()
    loads = panel_loads(pos_ref, first, got, x_ref, sem)
    for l in range(NL):
        sk_ref[l, WIDE:LANES, :] = jnp.zeros((LANES - WIDE, KS), bf16)
    for c in load_s:
        c.wait()
    stores = []
    for l in range(NL):
        for c in loads[l]:
            c.wait()
        for kz in range(4):
            t_ref[l, kz] = (
                jnp.dot(x_ref[l, kz].reshape(4 * ROWS, LANES), sk_ref[l], preferred_element_type=f32)
                .astype(bf16)
                .reshape(4, ROWS, KS)
            )
            if l == 0:
                stores.append(pltpu.make_async_copy(t_ref.at[0, kz], outs[kz], sem_out.at[kz]))
                stores[-1].start()
                continue
            for k in range(4):
                stores.append(
                    pltpu.make_async_copy(t_ref.at[1, kz, k], outs[4 + k].at[kz], sem_out.at[4 + 4 * kz + k])
                )
                stores[-1].start()
    for c in stores:
        c.wait()


def back_products(pos, got1, got2, sks):
    outs = pl.pallas_call(
        back_kernel,
        in_specs=[SMEM] + [HBM] * 22,
        out_specs=[HBM] * 8,
        out_shape=[jax.ShapeDtypeStruct((4, ROWS, KS), bf16)] * 8,
        scratch_shapes=[
            pltpu.VMEM((NL, 4, 4, ROWS, LANES), bf16),
            pltpu.VMEM((NL, LANES, KS), bf16),
            pltpu.VMEM((NL, 4, 4, ROWS, KS), bf16),
            pltpu.SemaphoreType.DMA((16,)),
            pltpu.SemaphoreType.DMA((8,)),
            pltpu.SemaphoreType.DMA((20,)),
        ],
        compiler_params=params(),
        cost_estimate=cost(16_000_000, 4_400_000_000),
    )(pos, *flat(got1, FIRST), *moved(got2), *flat(sks))
    return [list(outs[:4]), list(outs[4:])]


def owner_kernel(me_ref, got_ref, ranks_ref, _, mine_ref, scores_ref):
    total = jnp.sum(got_ref[...].astype(f32), axis=0)
    row = me_ref[0] * 8 + lax.broadcasted_iota(jnp.int32, (8, 128), 0)
    lane = lax.broadcasted_iota(jnp.int32, (8, 128), 1)
    my_rows = me_ref[0] * 8 + lax.broadcasted_iota(jnp.int32, (8, RANK), 0)
    owned, scores = [], 0.0
    for l in range(NL):
        diag = total[8 * l : 8 * l + 4, KS:] + total[8 * l + 4 : 8 * l + 8, KS:]
        scores = scores + diag
        trace = jnp.sum(jnp.sum(diag, axis=1, keepdims=True), axis=0, keepdims=True)
        mine = jnp.zeros((8, 128), f32)
        for c in range(4):
            mine = mine + jnp.where(lane + 128 * c == row, diag[c : c + 1, :], 0.0)
        my_diag = jnp.sum(mine, axis=1, keepdims=True)
        scale = 0.5 * KS / trace
        rms = jnp.sqrt(trace / (FF * KS))
        gram = total[8 * l : 8 * l + 8, 0:RANK]
        corrected = jnp.where(my_rows == ranks_ref[l : l + 1, :], 1.5 - scale * my_diag, -scale * gram)
        owned.append(jnp.concatenate([corrected / rms, total[8 * l : 8 * l + 8, RANK:KS]], 1))
    mine_ref[...] = jnp.broadcast_to(jnp.concatenate(owned, 0).astype(bf16)[None], (N, 16, KS))
    scores_ref[...] = scores / FF


def owner_rows(me, got, ranks, earlier):
    return pl.pallas_call(
        owner_kernel,
        in_specs=[SMEM, INNER, INNER, HBM],
        out_specs=[INNER, INNER],
        out_shape=[jax.ShapeDtypeStruct((N, 16, KS), bf16), jax.ShapeDtypeStruct((4, 128), f32)],
        compiler_params=params(),
        cost_estimate=cost(2_500_000),
    )(me, got, ranks, earlier)


def moments_kernel(rows_ref, sk0_ref, sk1_ref, one_ref, two_ref, basis_ref, first_ref, second_ref, factor_ref):
    rows = rows_ref[...].astype(f32)
    for l in range(NL):
        both = rows[:, 8 * l : 8 * l + 8, :].reshape(KS, KS).astype(bf16)
        factor, inner = both[:, :RANK], both[:, RANK:]
        factor_ref[l] = factor
        sk = (sk0_ref, sk1_ref)[l][...]
        basis_ref[l] = jnp.dot(sk, factor, preferred_element_type=f32).astype(bf16)
        correlation = lax.dot_general(
            inner, factor, (((0,), (0,)), ((), ())), preferred_element_type=f32
        ) / math.sqrt(FF * RANK)
        first_ref[l] = jnp.dot(one_ref[l], correlation, precision=highest, preferred_element_type=f32)
        second_ref[l] = jnp.dot(
            two_ref[l], correlation * correlation, precision=highest, preferred_element_type=f32
        )


def moments(rows, sk, one, two):
    return pl.pallas_call(
        moments_kernel,
        in_specs=[INNER] * 5,
        out_specs=[INNER] * 4,
        out_shape=[
            jax.ShapeDtypeStruct((NL, COLS, RANK), bf16),
            jax.ShapeDtypeStruct((NL, ROWS, RANK), f32),
            jax.ShapeDtypeStruct((NL, ROWS, RANK), f32),
            jax.ShapeDtypeStruct((NL, KS, RANK), bf16),
        ],
        compiler_params=params(),
        cost_estimate=cost(4_000_000, 500_000_000),
    )(rows, *sk, one, two)


def project_kernel(*refs):
    got = unflat(refs[:8])
    factor_ref, out_ref = refs[8:]
    for l in range(NL):
        t_rows = sum(got[l][k][...].astype(f32) for k in range(4))
        out_ref[l] = (
            jnp.dot(t_rows, factor_ref[l].astype(f32), precision=highest, preferred_element_type=f32)
            / math.sqrt(FF)
        ).astype(bf16)


def project(got, factor):
    return pl.pallas_call(
        project_kernel,
        in_specs=[INNER] * 9,
        out_specs=INNER,
        out_shape=jax.ShapeDtypeStruct((NL, ROWS, RANK), bf16),
        compiler_params=params(),
        cost_estimate=cost(2_000_000, 100_000_000),
    )(*flat(got), factor)


def reduce_kernel(*refs):
    got = unflat(refs[:8])
    outs = refs[8:]
    for l in range(NL):
        for k in range(4):
            outs[4 * l + k][...] = sum(got[l][j][k].astype(f32) for j in range(4)).astype(bf16)


def reduce_stage(got):
    outs = pl.pallas_call(
        reduce_kernel,
        in_specs=[INNER] * 8,
        out_specs=[INNER] * 8,
        out_shape=[jax.ShapeDtypeStruct((ROWS, KS), bf16)] * 8,
        compiler_params=params(),
        cost_estimate=cost(3_300_000),
    )(*flat(got))
    return [list(outs[:4]), list(outs[4:])]


def shift_back(bufs, stage):
    got = [[b[0], None, None, None] for b in bufs]
    for l, k in ISSUE:
        got[l][k] = shifted(bufs[l][4 - k], ORDERS[l][stage], k)
    return got


def shards(gradients, sketch, rank_lists, old_basis, first_moment, second_moment):
    s_rows = [lax.all_gather(sketch, axes, axis=0) for axes in (("z", "x"), ("z", "y"))]
    pos = jnp.stack([lax.axis_index(a) for a in AX]).astype(jnp.int32)
    got1 = permute_stage(pack(pos, gradients), 0, FIRST)
    got2 = permute_stage(second(pos, got1), 1)
    picker = (lax.broadcasted_iota(jnp.int32, (NL, KS, RANK), 1) == rank_lists[:, None, :]).astype(bf16)
    parts = shift_back(panel_products(pos, got1, got2, s_rows), 2)
    sketched, send = gram_products(parts, old_basis, picker)
    got = lax.all_to_all(send, AX, 0, 0, tiled=True)
    sks = permute_stage([[sk] * 4 for sk in sketched], 2)
    me = (16 * pos[0] + 4 * pos[1] + pos[2])[None]
    mine, scores = owner_rows(me, got, rank_lists, sks[1][1])
    everyone = lax.all_to_all(mine, AX, 0, 0, tiled=True)
    basis, first, second_out, factor = moments(everyone, sketched, first_moment, second_moment)
    back = shift_back(back_products(pos, got1, got2, sks), 0)
    back = shift_back(reduce_stage(back), 1)
    projected = project(back, factor)
    scores = scores + lax.ppermute(scores, "layer", [(0, 1), (1, 0)])
    return basis, projected, first, second_out, scores.reshape(KS)


def solution(mesh):
    cube = Mesh(mesh.devices.reshape(4, 4, 4, 2), AX + ("layer",))
    rows = P("layer", AX, None)
    return jax.shard_map(
        shards,
        mesh=cube,
        in_specs=(rows, P(AX, None), P("layer", None), rows, rows, rows),
        out_specs=(rows, rows, rows, rows, P()),
        check_vma=False,
    )
```
